32 devices in a mesh: space: 8 (over z, core), date: 4 (over y, x).
Axes of the slice: x: 2, y: 2, z: 4, core: 2. Of those that a mesh axis runs over, the one named last changes fastest.
Arguments:
- acquisitions: bfloat16 [2, 160, 7, 1024], P(None, 'date', None, 'space'), may hold values from -80 to 80
- acquisition_day: int32 [160], replicated, may hold values from 0 to 1428, as said below
Outputs:
- linked: float32 [2, 160, 1024], P(None, 'date', 'space')
The draws below stay inside these ranges and needn't reach their ends.
Inputs may be any that keep to these rules, and one draw needn't show every extreme that they name: `acquisition_day`: starts at 0 and rises by 6 or 12 days from one date to the next; (159) // 2 of the steps are 12 days.
All inputs are finite; a program needn't handle non-finite values.
Results may differ from the reference program's by a relative error of at most 0.0003.
Values may be sent and summed in bfloat16 or wider, within the bound.
No kernel may reach another device: no remote copies, remote signals or barrier semaphores. Data moves between devices by JAX's collectives and lax.ppermute only.
A program may use at most 64 MiB of HBM per device.

```python
import math
import jax
import jax.numpy as jnp
from jax import lax

DATES = 160
RIM = 10
LINES_IN = 7
ITERS = 2
POWER = 4
RANGE_DEV = 128
RANGE = 1024
N_SPACE = 8
N_DATE = 4


def draw_acquisitions(key, part):
    key = jax.random.fold_in(key, 11)
    keys = jax.random.split(key, 6)
    shape = (DATES, LINES_IN, RANGE)
    pixel_gain = jnp.exp(jax.random.uniform(keys[0], (1, LINES_IN, RANGE), jnp.float32, math.log(0.3), math.log(3.0)))
    date_gain = jnp.exp(jax.random.uniform(keys[1], (DATES, 1, 1), jnp.float32, math.log(0.3), math.log(3.0)))
    noise_real = jax.random.truncated_normal(keys[2], -4.0, 4.0, shape, jnp.float32) * 0.7071
    noise_imag = jax.random.truncated_normal(keys[3], -4.0, 4.0, shape, jnp.float32) * 0.7071
    signal = 0.25
    common = jax.random.uniform(keys[4], (DATES, 1, 1), jnp.float32, -math.pi, math.pi)
    jitter = jax.random.uniform(keys[5], shape, jnp.float32, -0.6, 0.6)
    phase = common + jitter
    gain = pixel_gain * date_gain
    real_part = gain * (signal * jnp.cos(phase) + noise_real)
    imag_part = gain * (signal * jnp.sin(phase) + noise_imag)
    return jnp.stack([real_part, imag_part]).astype(jnp.bfloat16)


def draw_acquisition_day(key, part):
    key = jax.random.fold_in(key, 23)
    order = jax.random.permutation(key, DATES - 1)
    longer = (order < (DATES - 1) // 2).astype(jnp.int32)
    gaps = 6 + 6 * longer
    gaps = jnp.concatenate([jnp.zeros((1,), jnp.int32), gaps])
    return jnp.cumsum(gaps).astype(jnp.int32)


def setup_inputs(seed: int = 0) -> dict:
    key_of = jax.random.split(jax.random.key(seed), 3)
    return {
        "acquisitions": draw_acquisitions(jax.random.fold_in(key_of[2], 71), 0),
        "acquisition_day": draw_acquisition_day(jax.random.fold_in(key_of[2], 71), 0),
    }


epsilon = 1e-06
reweight_gain = 4.0
taper_days = 360.0

def box_range(field, width):
    total = field[..., 0:width]
    for offset in range(1, 2 * RIM + 1):
        total = total + field[..., offset:offset + width]
    return total

def pixel_weight(intensity_sum):
    return 1.0 / (intensity_sum / DATES + epsilon)

def power_sums(panel, weight, width):
    values = panel.astype(jnp.float32)
    intensity = (values[0] * values[0] + values[1] * values[1]) * weight
    return box_range(lax.optimization_barrier(jnp.sum(intensity, axis=1)), width)

def coherence_block(rows, columns, weight, width, row_power, column_power, row_days, column_days):
    rows_scaled = rows.astype(jnp.float32) * weight
    columns_float = columns.astype(jnp.float32)
    real_sum = None
    imag_sum = None
    for line in range(rows.shape[2]):
        left_real = rows_scaled[0, :, line][:, None, :]
        left_imag = rows_scaled[1, :, line][:, None, :]
        right_real = columns_float[0, :, line][None]
        right_imag = columns_float[1, :, line][None]
        real_term = left_real * right_real + left_imag * right_imag
        imag_term = left_imag * right_real - left_real * right_imag
        real_sum = real_term if real_sum is None else real_sum + real_term
        imag_sum = imag_term if imag_sum is None else imag_sum + imag_term
    taper = jnp.exp(-jnp.abs(row_days[:, None] - column_days[None, :]) / taper_days)
    factor = taper[:, :, None] * lax.rsqrt(row_power + epsilon)[:, None, :] * lax.rsqrt(column_power + epsilon)[None, :, :]
    return jnp.stack([box_range(real_sum, width) * factor, box_range(imag_sum, width) * factor])

def full_coherence(panel, weight, days, width, block):
    dates = panel.shape[1]
    power = power_sums(panel, weight, width)

    def add_rows(index, coherence):
        first = (index * block).astype(jnp.int32)
        rows = lax.dynamic_slice_in_dim(panel, first, block, 1)
        part_power = lax.dynamic_slice_in_dim(power, first, block, 0)
        part_days = lax.dynamic_slice_in_dim(days, first, block, 0)
        piece = coherence_block(rows, panel, weight, width, part_power, power, part_days, days)
        return lax.dynamic_update_slice_in_dim(coherence, piece, first, 1)
    empty = jnp.zeros((2, dates, dates, width), jnp.float32)
    return lax.fori_loop(0, dates // block, add_rows, empty)

def apply_matrix(matrix, vector):
    real_part = lax.optimization_barrier(jnp.sum(matrix[0] * vector[0][None] - matrix[1] * vector[1][None], axis=1))
    imag_part = lax.optimization_barrier(jnp.sum(matrix[0] * vector[1][None] + matrix[1] * vector[0][None], axis=1))
    return jnp.stack([real_part, imag_part])

def reweight(coherence, rows, columns):
    row_length = jnp.sqrt(rows[0] * rows[0] + rows[1] * rows[1])
    column_length = jnp.sqrt(columns[0] * columns[0] + columns[1] * columns[1])
    magnitude = jnp.sqrt(coherence[0] * coherence[0] + coherence[1] * coherence[1])
    along_real = coherence[0] * columns[0][None] - coherence[1] * columns[1][None]
    along_imag = coherence[0] * columns[1][None] + coherence[1] * columns[0][None]
    agree = rows[0][:, None] * along_real + rows[1][:, None] * along_imag
    spread = row_length[:, None] * column_length[None] * magnitude - agree
    return coherence / (1.0 + reweight_gain * spread)

def unit_local(vector):
    mean_square = lax.optimization_barrier(jnp.mean(vector[0] * vector[0] + vector[1] * vector[1], axis=0))
    return vector * lax.rsqrt(mean_square + epsilon)

def link_window(panel, days, width):
    values = panel.astype(jnp.float32)
    weight = pixel_weight(lax.optimization_barrier(jnp.sum(values[0] * values[0] + values[1] * values[1], axis=0)))
    coherence = full_coherence(panel, weight, days, width, DATES // N_DATE)
    power_scale = 1.0 / math.sqrt(DATES)
    linked = unit_local(lax.optimization_barrier(jnp.sum(coherence, axis=2)))
    for outer in range(ITERS):
        matrix = reweight(coherence, linked, linked)
        iterate = linked
        for inner in range(POWER):
            iterate = apply_matrix(matrix, iterate) * power_scale
        linked = unit_local(iterate)
    return linked

def reference(acquisitions, acquisition_day):
    days = acquisition_day.astype(jnp.float32)
    padded = jnp.pad(acquisitions, ((0, 0), (0, 0), (0, 0), (RIM, RIM)))

    def one_range(index):
        start = (index * RANGE_DEV).astype(jnp.int32)
        panel = lax.dynamic_slice_in_dim(padded, start, RANGE_DEV + 2 * RIM, 3)
        return link_window(panel, days, RANGE_DEV)
    blocks = lax.map(one_range, jnp.arange(N_SPACE, dtype=jnp.int32))
    return jnp.moveaxis(blocks, 0, 2).reshape(2, DATES, RANGE)
```

```python
import functools
import math

import jax
import jax.numpy as jnp
from jax import lax
from jax.experimental import pallas as pl
from jax.experimental.pallas import tpu as pltpu
from jax.sharding import PartitionSpec as P

DATES = 160
RIM = 10
LINES = 7
ITERS = 2
POWER = 4
LANES = 128
PART = 256

epsilon = 1e-06
reweight_gain = 4.0
taper_days = 360.0

f32 = jnp.float32
bf16 = jnp.bfloat16
VMEM = pl.BlockSpec(memory_space=pltpu.VMEM)


class Plan:
    def __init__(self, shape, n_date):
        self.n_date = n_date
        self.own = shape[1]
        self.width = shape[3]
        self.cols = self.width // n_date
        self.pix = min(16, self.cols)
        self.halves = self.cols // self.pix
        self.groups = LANES // self.pix
        self.blocks = DATES // self.groups
        self.span = self.pix + 2 * RIM
        self.left = [d for d in range(n_date) if d * self.cols < RIM]
        self.right = [d for d in range(n_date) if (d + 1) * self.cols + RIM > self.width]


def pack_kernel(plan, x_ref, *refs):
    n_date, width, span = plan.n_date, plan.width, plan.span
    main, halo, plane = refs[:n_date], refs[n_date : 2 * n_date], refs[2 * n_date]
    me = lax.axis_index("date")
    for part in range(2):
        plane[part, :, 0:LINES, :] = x_ref[part].astype(f32)
    lane = lax.broadcasted_iota(jnp.int32, (1, LANES), 1)

    def place(first, low, high):
        tiles = [[jnp.zeros((plan.own, LANES), f32) for _ in range(PART // LANES)] for _ in range(2)]
        for line in range(LINES):
            start = line * span
            shift = lax.rem(start - first + 4 * LANES, LANES)
            for part in range(2):
                moved = pltpu.roll(plane[part, :, line, :], shift, 1)
                for tile in range(PART // LANES):
                    at = lane + tile * LANES - start
                    if start < (tile + 1) * LANES and start + span > tile * LANES:
                        inside = (at >= low) & (at < high)
                        tiles[part][tile] = jnp.where(inside, moved, tiles[part][tile])
        return [tile.astype(bf16) for part in tiles for tile in part]

    for r in range(n_date):
        dest = lax.rem(me + r, n_date)
        for half in range(plan.halves):
            first = dest * plan.cols + half * plan.pix - RIM
            low = jnp.maximum(0, -first)
            high = jnp.minimum(span, width - first)
            for k, tile in enumerate(place(first, low, high)):
                main[r][:, half * 2 * PART + k * LANES : half * 2 * PART + (k + 1) * LANES] = tile
        to_right = dest <= plan.left[-1]
        first = jnp.where(
            to_right,
            dest * plan.cols - RIM + width,
            dest * plan.cols + (plan.halves - 1) * plan.pix - RIM - width,
        )
        low = jnp.maximum(0, -first)
        high = jnp.minimum(span, width - first)
        for k, tile in enumerate(place(first, low, high)):
            halo[r][:, k * LANES : (k + 1) * LANES] = tile


def group_sum(x, pix):
    step = LANES // 2
    while step >= pix:
        x = x + pltpu.roll(x, step, 1)
        step //= 2
    return x


def link_kernel(plan, *refs):
    n_date, own, pix, halves = plan.n_date, plan.own, plan.pix, plan.halves
    groups, blocks = plan.groups, plan.blocks
    main, halo = refs[:n_date], refs[n_date : 2 * n_date]
    mask_ref, rep_ref, days_ref, out_ref = refs[2 * n_date : 2 * n_date + 4]
    (s_ref, left_ref, high_ref, low_ref, a_ref, raw_ref, cr_ref, ci_ref, ca_ref,
     mr_ref, mi_ref, ms_ref, y_ref, v_ref, ty_ref, tv_ref) = refs[2 * n_date + 4 :]
    me = lax.axis_index("date")
    nt = (((1,), (1,)), ((), ()))
    rows = [slice(b, b + 40) for b in range(0, DATES, 40)]
    sub = lax.broadcasted_iota(jnp.int32, (groups, LANES), 0)
    lane = lax.broadcasted_iota(jnp.int32, (groups, LANES), 1)
    diag = jnp.where(lane // pix == sub, 1.0, 0.0).astype(f32)

    def to_rows(y):
        return [
            jnp.sum(y[b * groups : (b + 1) * groups] * diag, axis=0, keepdims=True) for b in range(blocks)
        ]

    is_left = (me <= plan.left[-1]).astype(f32)
    is_right = (me >= plan.right[0]).astype(f32)
    for r in range(n_date):
        block = slice(r * own, (r + 1) * own)
        edge = halo[r][...].astype(f32)
        for h in range(halves):
            s = main[r][:, h * 2 * PART : (h + 1) * 2 * PART].astype(f32)
            if h == 0:
                s = s + edge * is_left
            if h == halves - 1:
                s = s + edge * is_right
            s_ref[h, block, :] = s

    grow = jnp.exp(days_ref[...] * (1.0 / taper_days))
    decay = jnp.exp(days_ref[...] * (-1.0 / taper_days))
    for h in range(halves):
        sr, si = s_ref[h, :, 0:PART], s_ref[h, :, PART : 2 * PART]
        left_ref[h, 0:DATES, 0:PART] = sr.astype(bf16)
        left_ref[h, 0:DATES, PART : 2 * PART] = si.astype(bf16)
        left_ref[h, DATES : 2 * DATES, 0:PART] = si.astype(bf16)
        left_ref[h, DATES : 2 * DATES, PART : 2 * PART] = (-sr).astype(bf16)
        intensity = sr * sr + si * si
        weight = 1.0 / (jnp.sum(intensity, axis=0, keepdims=True) / DATES + epsilon)
        for part, s in enumerate((sr, si)):
            at = slice(part * PART, (part + 1) * PART)
            scaled = s * weight
            high = scaled.astype(bf16).astype(f32)
            high_ref[h, :, at] = high
            low_ref[h, :, at] = scaled - high
        weighted = intensity * weight
        high = weighted.astype(bf16)
        low = (weighted - high.astype(f32)).astype(bf16)
        power = lax.dot_general(high, rep_ref[...], nt, preferred_element_type=f32)
        power = power + lax.dot_general(low, rep_ref[...], nt, preferred_element_type=f32)
        root = lax.rsqrt(power + epsilon)
        for k, t in enumerate((grow, decay)):
            y = t * root
            ty_ref[k, h] = y
            for b, row in enumerate(to_rows(y)):
                tv_ref[k, h, b : b + 1, :] = row

    per = 2 if blocks % 2 == 0 else 1
    unit = max(1, 16 // pix)

    def build(h, first):
        for p in range(per):
            for g in range(0, groups, unit):
                for k, ref in enumerate((high_ref, low_ref)):
                    rows16 = jnp.concatenate(
                        [
                            jnp.broadcast_to(ref[h, pl.ds((first + p) * groups + g + u, 1), :], (pix, 2 * PART))
                            for u in range(unit)
                        ],
                        axis=0,
                    )
                    at = p * LANES + g * pix
                    a_ref[h, k, at : at + 16, :] = rows16.astype(bf16) * mask_ref[...]

    def multiply(h):
        total = lax.dot_general(left_ref[h], a_ref[h, 0], nt, preferred_element_type=f32)
        raw_ref[h] = total + lax.dot_general(left_ref[h], a_ref[h, 1], nt, preferred_element_type=f32)

    def normalise(h, first):
        for p in range(per):
            b = first + p
            grow_row = tv_ref[0, h, pl.ds(b, 1), :]
            decay_row = tv_ref[1, h, pl.ds(b, 1), :]
            at = slice(p * LANES, (p + 1) * LANES)
            for part in rows:
                shifted = slice(part.start + DATES, part.stop + DATES)
                factor = jnp.minimum(ty_ref[0, h, part] * decay_row, ty_ref[1, h, part] * grow_row)
                cr = raw_ref[h, part, at] * factor
                ci = raw_ref[h, shifted, at] * factor
                square = cr * cr + ci * ci
                cr_ref[h, b, part, :] = cr
                ci_ref[h, b, part, :] = ci
                ca_ref[h, b, part, :] = square * lax.rsqrt(jnp.maximum(square, 1e-36))
                y_ref[0, h, part] += cr
                y_ref[1, h, part] += ci

    y_ref[...] = jnp.zeros(y_ref.shape, f32)

    def coherence(step, carry):
        for h in range(halves):
            build(h, step * per)
        for h in range(halves):
            multiply(h)
        for h in range(halves):
            normalise(h, step * per)
        return carry

    lax.fori_loop(0, blocks // per, coherence, 0)

    def unit_vector(scale, times):
        for h in range(halves):
            yr = group_sum(y_ref[0, h], pix) * scale
            yi = group_sum(y_ref[1, h], pix) * scale
            mean = jnp.sum(yr * yr + yi * yi, axis=0, keepdims=True) / DATES
            inv = lax.rsqrt(mean + epsilon)
            yr, yi = yr * inv, yi * inv
            y_ref[0, h] = yr
            y_ref[1, h] = yi

    def as_rows():
        for h in range(halves):
            for k in range(3):
                for b, row in enumerate(to_rows(y_ref[k, h])):
                    v_ref[k, h, b : b + 1, :] = row

    def first_step():
        for h in range(halves):
            yr, yi = y_ref[0, h], y_ref[1, h]
            square = yr * yr + yi * yi
            y_ref[2, h] = square * lax.rsqrt(jnp.maximum(square, 1e-36))
        as_rows()

        def body(b, carry):
            for h in range(halves):
                lr, li = v_ref[0, h, pl.ds(b, 1), :], v_ref[1, h, pl.ds(b, 1), :]
                la = v_ref[2, h, pl.ds(b, 1), :] * reweight_gain
                lr4, li4 = lr * reweight_gain, li * reweight_gain
                sum_r = jnp.zeros((8, LANES), f32)
                sum_i = jnp.zeros((8, LANES), f32)
                for part in rows:
                    cr, ci = cr_ref[h, b, part, :], ci_ref[h, b, part, :]
                    yr, yi = y_ref[0, h, part], y_ref[1, h, part]
                    pr = cr * yr + ci * yi
                    pi = cr * yi - ci * yr
                    den = (1.0 + ca_ref[h, b, part, :] * (y_ref[2, h, part] * la)) - (lr4 * pr + li4 * pi)
                    g = 1.0 / den
                    mr, mi = cr * g, ci * g
                    mr_ref[h, b, part, :] = mr
                    mi_ref[h, b, part, :] = mi
                    ms_ref[h, b, part, :] = mr + mi
                    sum_r = sum_r + jnp.sum((pr * g).reshape(5, 8, LANES), axis=0)
                    sum_i = sum_i + jnp.sum((pi * g).reshape(5, 8, LANES), axis=0)
                set_row(h, b, jnp.sum(sum_r, axis=0, keepdims=True), jnp.sum(sum_i, axis=0, keepdims=True))
            return carry

        lax.fori_loop(0, blocks, body, 0)

    def set_row(h, b, vr, vi):
        tv_ref[0, h, pl.ds(b, 1), :] = vr
        tv_ref[1, h, pl.ds(b, 1), :] = vi

    def rows_to_lanes():
        for h in range(halves):
            vr, vi = tv_ref[0, h], tv_ref[1, h]
            v_ref[0, h] = vr
            v_ref[1, h] = vi - vr
            v_ref[2, h] = vr + vi
        for h in range(halves):
            for part in rows:
                zero = jnp.zeros((40, LANES), f32)

                def body(b, acc, h=h, part=part):
                    v0, v1, v2 = (v_ref[k, h, pl.ds(b, 1), :] for k in range(3))
                    return (
                        acc[0] + ms_ref[h, b, part, :] * v0,
                        acc[1] + mr_ref[h, b, part, :] * v1,
                        acc[2] + mi_ref[h, b, part, :] * v2,
                    )

                k1, k2, k3 = lax.fori_loop(0, blocks, body, (zero, zero, zero), unroll=5)
                y_ref[0, h, part] = k1 - k3
                y_ref[1, h, part] = k1 + k2

    def lanes_to_rows():
        for h in range(halves):
            yr = group_sum(y_ref[0, h], pix)
            yi = group_sum(y_ref[1, h], pix)
            y_ref[0, h] = yr
            y_ref[1, h] = yi - yr
            y_ref[2, h] = yr + yi
        for h in range(halves):

            def body(step, carry, h=h):
                sums = [[jnp.zeros((8, LANES), f32) for _ in range(3)] for _ in range(per)]
                for part in rows:
                    y0, y1, y2 = (y_ref[k, h, part] for k in range(3))
                    for p in range(per):
                        b = step * per + p
                        for k, (m, y) in enumerate(((ms_ref, y0), (mi_ref, y1), (mr_ref, y2))):
                            sums[p][k] += jnp.sum((m[h, b, part, :] * y).reshape(5, 8, LANES), axis=0)
                for p in range(per):
                    k1, k2, k3 = (jnp.sum(s, axis=0, keepdims=True) for s in sums[p])
                    set_row(h, step * per + p, k1 + k2, k3 - k1)
                return carry

            lax.fori_loop(0, blocks // per, body, 0, unroll=2 if blocks // per % 2 == 0 else 1)

    unit_vector(1.0, 1.0)
    for outer in range(ITERS):
        first_step()
        for step in range(1, POWER):
            if step % 2:
                rows_to_lanes()
            else:
                lanes_to_rows()
        unit_vector(1.0 / math.sqrt(DATES) ** POWER, 1.0)

    spread = lax.broadcasted_iota(jnp.int32, (1, LANES), 1) // pix % halves
    for k in range(2):
        value = y_ref[k, 0]
        for h in range(1, halves):
            value = jnp.where(spread == h, y_ref[k, h], value)
        out_ref[k] = value


def local(acquisitions, acquisition_day):
    n_date, n_space = lax.axis_size("date"), lax.axis_size("space")
    plan = Plan(acquisitions.shape, n_date)
    own, pix, halves, groups, blocks = plan.own, plan.pix, plan.halves, plan.groups, plan.blocks
    me = lax.axis_index("date")

    packed = pl.pallas_call(
        functools.partial(pack_kernel, plan),
        out_shape=[jax.ShapeDtypeStruct((own, halves * 2 * PART), bf16)] * n_date
        + [jax.ShapeDtypeStruct((own, 2 * PART), bf16)] * n_date,
        in_specs=[VMEM],
        out_specs=[VMEM] * (2 * n_date),
        scratch_shapes=[pltpu.VMEM((2, own, 8, LANES), f32)],
        compiler_params=pltpu.CompilerParams(vmem_limit_bytes=32 * 2**20),
    )(acquisitions)
    main, halo = list(packed[:n_date]), list(packed[n_date:])
    for r in range(1, n_date):
        main[r] = lax.ppermute(main[r], "date", [(i, (i + r) % n_date) for i in range(n_date)])
    for r in range(n_date):
        pairs = []
        for s in range(n_space):
            for k in range(n_date):
                d = (k + r) % n_date
                if d in plan.left and s + 1 < n_space:
                    pairs.append((s * n_date + k, (s + 1) * n_date + d))
                if d in plan.right and s > 0:
                    pairs.append((s * n_date + k, (s - 1) * n_date + d))
        halo[r] = lax.ppermute(halo[r], ("space", "date"), pairs)

    lanes = jnp.arange(PART)
    line, column = lanes // plan.span, lanes % plan.span
    offset = column[None, :] - jnp.arange(pix)[:, None]
    inside = (line < LINES)[None, :] & (offset >= 0) & (offset <= 2 * RIM)
    mask = jnp.tile(inside.astype(bf16), (16 // pix, 2))
    rep = jnp.tile(inside.astype(bf16), (groups, 1))
    order = lax.rem(me + n_date - jnp.arange(n_date), n_date)
    days = acquisition_day.astype(f32).reshape(n_date, own)[order].reshape(DATES, 1)
    days = jnp.broadcast_to(days, (DATES, LANES))

    matrix = pltpu.VMEM((halves, blocks, DATES, LANES), f32)
    per = 2 if blocks % 2 == 0 else 1
    out = pl.pallas_call(
        functools.partial(link_kernel, plan),
        out_shape=jax.ShapeDtypeStruct((2, DATES, LANES), f32),
        in_specs=[VMEM] * (2 * n_date + 3),
        out_specs=VMEM,
        scratch_shapes=[
            pltpu.VMEM((halves, DATES, 2 * PART), f32),
            pltpu.VMEM((halves, 2 * DATES, 2 * PART), bf16),
            pltpu.VMEM((halves, DATES, 2 * PART), f32),
            pltpu.VMEM((halves, DATES, 2 * PART), f32),
            pltpu.VMEM((halves, 2, per * LANES, 2 * PART), bf16),
            pltpu.VMEM((halves, 2 * DATES, per * LANES), f32),
        ]
        + [matrix] * 6
        + [
            pltpu.VMEM((3, halves, DATES, LANES), f32),
            pltpu.VMEM((3, halves, blocks, LANES), f32),
            pltpu.VMEM((2, halves, DATES, LANES), f32),
            pltpu.VMEM((2, halves, blocks, LANES), f32),
        ],
        compiler_params=pltpu.CompilerParams(vmem_limit_bytes=56 * 2**20),
    )(*main, *halo, mask, rep, days)

    lane_owner = jnp.arange(LANES) // plan.cols
    result = out[:, 0:own]
    for r in range(1, n_date):
        piece = out[:, r * own : (r + 1) * own]
        piece = lax.ppermute(piece, "date", [(i, (i - r) % n_date) for i in range(n_date)])
        result = jnp.where(lane_owner == lax.rem(me + r, n_date), piece, result)
    return result


def solution(mesh):
    return jax.shard_map(
        local,
        mesh=mesh,
        in_specs=(P(None, "date", None, "space"), P()),
        out_specs=P(None, "date", "space"),
        check_vma=False,
    )
```

```python
import functools
import math

import jax
import jax.numpy as jnp
from jax import lax
from jax.experimental import pallas as pl
from jax.experimental.pallas import tpu as pltpu
from jax.sharding import PartitionSpec as P

DATES = 160
RIM = 10
LINES = 7
ITERS = 2
POWER = 4
LANES = 128
PART = 256

epsilon = 1e-06
reweight_gain = 4.0
taper_days = 360.0

f32 = jnp.float32
bf16 = jnp.bfloat16
VMEM = pl.BlockSpec(memory_space=pltpu.VMEM)


class Plan:
    def __init__(self, shape, n_date):
        self.n_date = n_date
        self.own = shape[1]
        self.width = shape[3]
        self.cols = self.width // n_date
        self.pix = min(16, self.cols)
        self.halves = self.cols // self.pix
        assert self.halves <= 2
        self.groups = LANES // self.pix
        self.blocks = DATES // self.groups
        self.per = 2 if self.blocks % 2 == 0 else 1
        self.span = self.pix + 2 * RIM
        self.left = [d for d in range(n_date) if d * self.cols < RIM]
        self.right = [n_date - 1 - d for d in self.left]
        self.message = self.halves * 2 * PART + PART

    def half(self, dest, slot):
        if self.halves == 1:
            return 0
        return jnp.where(dest <= self.left[-1], 1 - slot, slot)


def pack_kernel(plan, x_ref, *refs):
    n_date, width, span = plan.n_date, plan.width, plan.span
    main, plane = refs[:n_date], refs[n_date]
    me = lax.axis_index("date")
    plane[...] = x_ref[...].astype(f32)
    lane = lax.broadcasted_iota(jnp.int32, (1, LANES), 1)
    tile_count = PART // LANES

    def place(tiles, part, first, low, high, lead=0):
        for line in range(LINES):
            start = line * span
            shift = lax.rem(start + lead - first + 4 * LANES, LANES)
            moved = pltpu.roll(plane[part, line], shift, 1)
            for tile in range(tile_count):
                if start - 16 < (tile + 1) * LANES and start + span + 16 > tile * LANES:
                    at = lane + (tile * LANES - start) - lead
                    tiles[tile] = jnp.where((at >= low) & (at < high), moved, tiles[tile])

    def blank():
        return [jnp.zeros((plan.own, LANES), f32) for _ in range(tile_count)]

    def put(r, base, tiles):
        for k, tile in enumerate(tiles):
            main[r][:, base + k * LANES : base + (k + 1) * LANES] = tile.astype(bf16)

    for r in range(n_date):
        dest = lax.rem(me + r, n_date)
        for slot in range(plan.halves):
            first = dest * plan.cols + plan.half(dest, slot) * plan.pix - RIM
            low = jnp.maximum(0, -first)
            high = jnp.minimum(span, width - first)
            for part in range(2):
                tiles = blank()
                place(tiles, part, first, low, high)
                put(r, (slot * 2 + part) * PART, tiles)
        other = n_date - 1 - dest
        after = dest >= plan.right[-1]
        first = jnp.where(after, other * plan.cols - RIM + width, (other + 1) * plan.cols - plan.pix - RIM - width)
        low = jnp.where(after, 0, jnp.maximum(0, -first))
        high = jnp.where(after, jnp.minimum(RIM, width - first), span)
        low = jnp.where(after, low, jnp.maximum(low, span - RIM))
        tiles = blank()
        place(tiles, 0, first, low, high)
        place(tiles, 1, first, low, high, jnp.where(after, RIM, -RIM))
        put(r, plan.halves * 2 * PART, tiles)


def group_sum(x, pix):
    step = LANES // 2
    while step >= pix:
        x = x + pltpu.roll(x, step, 1)
        step //= 2
    return x


def link_kernel(plan, slot, *refs):
    n_date, own, pix = plan.n_date, plan.own, plan.pix
    groups, blocks, per, span = plan.groups, plan.blocks, plan.per, plan.span
    last = slot == plan.halves - 1
    main, days_ref, refs = refs[:n_date], refs[n_date], refs[n_date + 1 :]
    edge_ref = before_ref = None
    if last:
        edge_ref, refs = refs[0], refs[1:]
        if slot:
            before_ref, refs = refs[0], refs[1:]
    outs, refs = refs[: n_date if last else 1], refs[n_date if last else 1 :]
    (s_ref, left_ref, high_ref, low_ref, a_ref, raw_ref, cr_ref, ci_ref, ca_ref,
     mr_ref, mi_ref, ms_ref, y_ref, v_ref, ty_ref, tv_ref) = refs
    me = lax.axis_index("date")
    nt = (((1,), (1,)), ((), ()))
    rows = [slice(b, b + 40) for b in range(0, DATES, 40)]
    sub = lax.broadcasted_iota(jnp.int32, (groups, LANES), 0)
    lane = lax.broadcasted_iota(jnp.int32, (groups, LANES), 1)
    diag = jnp.where(lane // pix == sub, 1.0, 0.0).astype(f32)

    column = lax.broadcasted_iota(jnp.int32, (16, PART), 1)
    for _line in range(1, LINES):
        column = jnp.where(column >= span, column - span, column)
    spot = lax.broadcasted_iota(jnp.int32, (16, PART), 1)
    offset = column - lax.rem(lax.broadcasted_iota(jnp.int32, (16, PART), 0), pix)
    inside = (offset >= 0) & (offset <= 2 * RIM) & (spot < LINES * span)
    inside = jnp.where(inside, 1.0, 0.0).astype(f32)
    mask = jnp.concatenate([inside, inside], axis=1).astype(bf16)
    rep = jnp.concatenate([inside] * (LANES // 16), axis=0).astype(bf16)

    def to_rows(y):
        return [
            jnp.sum(y[b * groups : (b + 1) * groups] * diag, axis=0, keepdims=True) for b in range(blocks)
        ]

    for r in range(n_date):
        s_ref[r * own : (r + 1) * own, :] = main[r][:, slot * 2 * PART : (slot + 1) * 2 * PART].astype(f32)
    if last:
        is_left = me <= plan.left[-1]
        is_edge = is_left | (me >= plan.right[-1])
        edge = edge_ref[...].astype(f32)
        raw_ref[0:DATES, 0:PART] = edge
        raw_ref[DATES : 2 * DATES, 0:PART] = edge

        @pl.when(is_edge)
        def _():
            start = lax.rem(3 * n_date - 1 - 2 * me, n_date) * own
            got = raw_ref[pl.ds(pl.multiple_of(start, 8), DATES), 0:PART]
            at = lax.broadcasted_iota(jnp.int32, (1, PART), 1)
            col = at
            for _line in range(1, LINES):
                col = jnp.where(col >= span, col - span, col)
            start = jnp.where(is_left, 0, span - RIM)
            valid = (col >= start) & (col < start + RIM) & (at < LINES * span)
            s_ref[:, 0:PART] = jnp.where(valid, s_ref[:, 0:PART] + got, s_ref[:, 0:PART])
            back = jnp.where(is_left, PART - RIM, RIM)
            got = pltpu.roll(got, back, 1)
            s_ref[:, PART : 2 * PART] = jnp.where(valid, s_ref[:, PART : 2 * PART] + got, s_ref[:, PART : 2 * PART])

    for r in range(n_date):
        first = lax.rem(me + n_date - r, n_date) * own
        for t in range(own):
            day = days_ref[first + t].astype(f32)
            y_ref[0, r * own + t : r * own + t + 1, :] = jnp.broadcast_to(day, (1, LANES))
    days = y_ref[0]
    grow = jnp.exp(days * (1.0 / taper_days))
    decay = jnp.exp(days * (-1.0 / taper_days))
    sr, si = s_ref[:, 0:PART], s_ref[:, PART : 2 * PART]
    left_ref[0:DATES, 0:PART] = sr.astype(bf16)
    left_ref[0:DATES, PART : 2 * PART] = si.astype(bf16)
    left_ref[DATES : 2 * DATES, 0:PART] = si.astype(bf16)
    left_ref[DATES : 2 * DATES, PART : 2 * PART] = (-sr).astype(bf16)
    intensity = sr * sr + si * si
    weight = 1.0 / (jnp.sum(intensity, axis=0, keepdims=True) / DATES + epsilon)
    for part, s in enumerate((sr, si)):
        at = slice(part * PART, (part + 1) * PART)
        scaled = s * weight
        high = scaled.astype(bf16).astype(f32)
        high_ref[:, at] = high
        low_ref[:, at] = scaled - high
    weighted = intensity * weight
    high = weighted.astype(bf16)
    low = (weighted - high.astype(f32)).astype(bf16)
    power = lax.dot_general(high, rep, nt, preferred_element_type=f32)
    power = power + lax.dot_general(low, rep, nt, preferred_element_type=f32)
    root = lax.rsqrt(power + epsilon)
    for k, t in enumerate((grow, decay)):
        y = t * root
        ty_ref[k] = y
        for b, row in enumerate(to_rows(y)):
            tv_ref[k, b : b + 1, :] = row

    unit = max(1, 16 // pix)

    def build(first):
        for p in range(per):
            for g in range(0, groups, unit):
                for k, ref in enumerate((high_ref, low_ref)):
                    rows16 = jnp.concatenate(
                        [
                            jnp.broadcast_to(ref[pl.ds((first + p) * groups + g + u, 1), :], (pix, 2 * PART))
                            for u in range(unit)
                        ],
                        axis=0,
                    )
                    at = p * LANES + g * pix
                    a_ref[k, at : at + 16, :] = rows16.astype(bf16) * mask

    def multiply():
        total = lax.dot_general(left_ref[...], a_ref[0], nt, preferred_element_type=f32)
        raw_ref[...] = total + lax.dot_general(left_ref[...], a_ref[1], nt, preferred_element_type=f32)

    def normalise(first):
        for p in range(per):
            b = first + p
            grow_row = tv_ref[0, pl.ds(b, 1), :]
            decay_row = tv_ref[1, pl.ds(b, 1), :]
            at = slice(p * LANES, (p + 1) * LANES)
            for part in rows:
                shifted = slice(part.start + DATES, part.stop + DATES)
                factor = jnp.minimum(ty_ref[0, part] * decay_row, ty_ref[1, part] * grow_row)
                cr = raw_ref[part, at] * factor
                ci = raw_ref[shifted, at] * factor
                square = cr * cr + ci * ci
                cr_ref[b, part, :] = cr
                ci_ref[b, part, :] = ci
                ca_ref[b, part, :] = square * lax.rsqrt(jnp.maximum(square, 1e-36))
                y_ref[0, part] += cr
                y_ref[1, part] += ci

    y_ref[...] = jnp.zeros(y_ref.shape, f32)

    def coherence(step, carry):
        build(step * per)
        multiply()
        normalise(step * per)
        return carry

    lax.fori_loop(0, blocks // per, coherence, 0)

    def unit_vector(scale):
        yr = group_sum(y_ref[0], pix) * scale
        yi = group_sum(y_ref[1], pix) * scale
        mean = jnp.sum(yr * yr + yi * yi, axis=0, keepdims=True) / DATES
        inv = lax.rsqrt(mean + epsilon)
        y_ref[0] = yr * inv
        y_ref[1] = yi * inv

    def first_step():
        yr, yi = y_ref[0], y_ref[1]
        square = yr * yr + yi * yi
        y_ref[2] = square * lax.rsqrt(jnp.maximum(square, 1e-36))
        for k in range(3):
            for b, row in enumerate(to_rows(y_ref[k])):
                v_ref[k, b : b + 1, :] = row

        def body(b, carry):
            la = v_ref[2, pl.ds(b, 1), :] * reweight_gain
            lr4 = v_ref[0, pl.ds(b, 1), :] * reweight_gain
            li4 = v_ref[1, pl.ds(b, 1), :] * reweight_gain
            sum_r = jnp.zeros((8, LANES), f32)
            sum_i = jnp.zeros((8, LANES), f32)
            for part in rows:
                cr, ci = cr_ref[b, part, :], ci_ref[b, part, :]
                yr, yi = y_ref[0, part], y_ref[1, part]
                pr = cr * yr + ci * yi
                pi = cr * yi - ci * yr
                den = (1.0 + ca_ref[b, part, :] * (y_ref[2, part] * la)) - (lr4 * pr + li4 * pi)
                g = 1.0 / den
                mr, mi = cr * g, ci * g
                mr_ref[b, part, :] = mr
                mi_ref[b, part, :] = mi
                ms_ref[b, part, :] = mr + mi
                sum_r = sum_r + jnp.sum((pr * g).reshape(5, 8, LANES), axis=0)
                sum_i = sum_i + jnp.sum((pi * g).reshape(5, 8, LANES), axis=0)
            set_row(b, jnp.sum(sum_r, axis=0, keepdims=True), jnp.sum(sum_i, axis=0, keepdims=True))
            return carry

        lax.fori_loop(0, blocks, body, 0)

    def set_row(b, vr, vi):
        tv_ref[0, pl.ds(b, 1), :] = vr
        tv_ref[1, pl.ds(b, 1), :] = vi

    def rows_to_lanes():
        vr, vi = tv_ref[0], tv_ref[1]
        v_ref[0] = vr
        v_ref[1] = vi - vr
        v_ref[2] = vr + vi
        for part in rows:
            zero = jnp.zeros((40, LANES), f32)

            def body(b, acc, part=part):
                v0, v1, v2 = (v_ref[k, pl.ds(b, 1), :] for k in range(3))
                return (
                    acc[0] + ms_ref[b, part, :] * v0,
                    acc[1] + mr_ref[b, part, :] * v1,
                    acc[2] + mi_ref[b, part, :] * v2,
                )

            k1, k2, k3 = lax.fori_loop(0, blocks, body, (zero, zero, zero), unroll=5)
            y_ref[0, part] = k1 - k3
            y_ref[1, part] = k1 + k2

    def lanes_to_rows():
        yr = group_sum(y_ref[0], pix)
        yi = group_sum(y_ref[1], pix)
        y_ref[0] = yr
        y_ref[1] = yi - yr
        y_ref[2] = yr + yi

        def body(step, carry):
            sums = [[jnp.zeros((8, LANES), f32) for _ in range(3)] for _ in range(per)]
            for part in rows:
                y0, y1, y2 = (y_ref[k, part] for k in range(3))
                for p in range(per):
                    b = step * per + p
                    for k, (m, y) in enumerate(((ms_ref, y0), (mi_ref, y1), (mr_ref, y2))):
                        sums[p][k] += jnp.sum((m[b, part, :] * y).reshape(5, 8, LANES), axis=0)
            for p in range(per):
                k1, k2, k3 = (jnp.sum(s, axis=0, keepdims=True) for s in sums[p])
                set_row(step * per + p, k1 + k2, k3 - k1)
            return carry

        lax.fori_loop(0, blocks // per, body, 0, unroll=2 if blocks // per % 2 == 0 else 1)

    unit_vector(1.0)
    for outer in range(ITERS):
        first_step()
        for step in range(1, POWER):
            if step % 2:
                rows_to_lanes()
            else:
                lanes_to_rows()
        unit_vector(1.0 / math.sqrt(DATES) ** POWER)

    if not last:
        outs[0][...] = y_ref[0:2]
        return
    place = lax.rem(lax.broadcasted_iota(jnp.int32, (1, LANES), 1) // pix, plan.halves)
    here = place == plan.half(me, slot)
    for r in range(n_date):
        at = slice(r * own, (r + 1) * own)
        for k in range(2):
            value = y_ref[k, at]
            if slot:
                value = jnp.where(here, value, before_ref[k, at])
            outs[r][k] = value


def link(plan, slot, main, days, *more):
    last = slot == plan.halves - 1
    matrix = pltpu.VMEM((plan.blocks, DATES, LANES), f32)
    samples = pltpu.VMEM((DATES, 2 * PART), f32)
    if last:
        shapes = [jax.ShapeDtypeStruct((2, plan.own, LANES), f32)] * plan.n_date
    else:
        shapes = [jax.ShapeDtypeStruct((2, DATES, LANES), f32)]
    return pl.pallas_call(
        functools.partial(link_kernel, plan, slot),
        out_shape=shapes,
        in_specs=[VMEM] * plan.n_date + [pl.BlockSpec(memory_space=pltpu.SMEM)] + [VMEM] * len(more),
        out_specs=[VMEM] * len(shapes),
        scratch_shapes=[
            samples,
            pltpu.VMEM((2 * DATES, 2 * PART), bf16),
            samples,
            samples,
            pltpu.VMEM((2, plan.per * LANES, 2 * PART), bf16),
            pltpu.VMEM((2 * DATES, PART), f32),
        ]
        + [matrix] * 6
        + [
            pltpu.VMEM((3, DATES, LANES), f32),
            pltpu.VMEM((3, plan.blocks, LANES), f32),
            pltpu.VMEM((2, DATES, LANES), f32),
            pltpu.VMEM((2, plan.blocks, LANES), f32),
        ],
        compiler_params=pltpu.CompilerParams(vmem_limit_bytes=24 * 2**20),
    )(*main, days, *more)


def local(acquisitions, acquisition_day):
    n_date, n_space = lax.axis_size("date"), lax.axis_size("space")
    plan = Plan(acquisitions.shape, n_date)
    own = plan.own
    me = lax.axis_index("date")

    main = pl.pallas_call(
        functools.partial(pack_kernel, plan),
        out_shape=[jax.ShapeDtypeStruct((own, plan.message), bf16)] * n_date,
        in_specs=[VMEM],
        out_specs=[VMEM] * n_date,
        scratch_shapes=[pltpu.VMEM((2, LINES, own, LANES), f32)],
        compiler_params=pltpu.CompilerParams(vmem_limit_bytes=24 * 2**20),
    )(jnp.transpose(acquisitions, (0, 2, 1, 3)))
    main = list(main)
    for r in range(1, n_date):
        main[r] = lax.ppermute(main[r], "date", [(i, (i + r) % n_date) for i in range(n_date)])
    swap = []
    for s in range(n_space - 1):
        for d in plan.left:
            before, after = s * n_date + n_date - 1 - d, (s + 1) * n_date + d
            swap += [(before, after), (after, before)]
    edge = jnp.concatenate([m[:, plan.halves * 2 * PART :] for m in main], axis=0)
    edge = lax.ppermute(edge, ("space", "date"), swap)

    if plan.halves == 1:
        out = link(plan, 0, main, acquisition_day, edge)
    else:
        (before,) = link(plan, 0, main, acquisition_day)
        out = link(plan, 1, main, acquisition_day, edge, before)

    lane_owner = jnp.arange(LANES) // plan.cols
    result = out[0]
    for r in range(1, n_date):
        piece = lax.ppermute(out[r], "date", [(i, (i - r) % n_date) for i in range(n_date)])
        result = jnp.where(lane_owner == lax.rem(me + r, n_date), piece, result)
    return result


def solution(mesh):
    return jax.shard_map(
        local,
        mesh=mesh,
        in_specs=(P(None, "date", None, "space"), P()),
        out_specs=P(None, "date", "space"),
        check_vma=False,
    )
```

```python
import functools
import math

import jax
import jax.numpy as jnp
from jax import lax
from jax.experimental import pallas as pl
from jax.experimental.pallas import tpu as pltpu
from jax.sharding import PartitionSpec as P

DATES = 160
RIM = 10
LINES = 7
ITERS = 2
POWER = 4
LANES = 128
PART = 256

epsilon = 1e-06
reweight_gain = 4.0
taper_days = 360.0

f32 = jnp.float32
bf16 = jnp.bfloat16
VMEM = pl.BlockSpec(memory_space=pltpu.VMEM)


class Plan:
    def __init__(self, shape, n_date):
        self.n_date = n_date
        self.own = shape[1]
        self.width = shape[3]
        self.cols = self.width // n_date
        self.pix = min(16, self.cols)
        self.halves = self.cols // self.pix
        assert self.halves <= 2
        self.groups = LANES // self.pix
        self.blocks = DATES // self.groups
        self.per = 2 if self.blocks % 2 == 0 else 1
        self.span = self.pix + 2 * RIM
        self.left = [d for d in range(n_date) if d * self.cols < RIM]
        self.right = [n_date - 1 - d for d in self.left]
        self.message = self.halves * 2 * PART + PART

    def chunk(self, date):
        odd = lax.rem(lax.axis_index("space"), 2) == 1
        return jnp.where(odd, self.n_date - 1 - date, date)

    def half(self, chunk, slot):
        if self.halves == 1:
            return 0
        return jnp.where(chunk <= self.left[-1], 1 - slot, slot)


def pack_kernel(plan, x_ref, *refs):
    n_date, width, span = plan.n_date, plan.width, plan.span
    main, plane = refs[:n_date], refs[n_date]
    me = lax.axis_index("date")
    plane[...] = x_ref[...].astype(f32)
    lane = lax.broadcasted_iota(jnp.int32, (1, LANES), 1)
    tile_count = PART // LANES

    def place(tiles, part, first, low, high, lead=0):
        for line in range(LINES):
            start = line * span
            shift = lax.rem(start + lead - first + 4 * LANES, LANES)
            moved = pltpu.roll(plane[part, line], shift, 1)
            for tile in range(tile_count):
                if start - 16 < (tile + 1) * LANES and start + span + 16 > tile * LANES:
                    at = lane + (tile * LANES - start) - lead
                    tiles[tile] = jnp.where((at >= low) & (at < high), moved, tiles[tile])

    def blank():
        return [jnp.zeros((plan.own, LANES), f32) for _ in range(tile_count)]

    def put(r, base, tiles):
        for k, tile in enumerate(tiles):
            main[r][:, base + k * LANES : base + (k + 1) * LANES] = tile.astype(bf16)

    for r in range(n_date):
        chunk = plan.chunk(lax.rem(me + r, n_date))
        for slot in range(plan.halves):
            first = chunk * plan.cols + plan.half(chunk, slot) * plan.pix - RIM
            low = jnp.maximum(0, -first)
            high = jnp.minimum(span, width - first)
            for part in range(2):
                tiles = blank()
                place(tiles, part, first, low, high)
                put(r, (slot * 2 + part) * PART, tiles)
        other = n_date - 1 - chunk
        after = chunk >= plan.right[-1]
        first = jnp.where(after, other * plan.cols - RIM + width, (other + 1) * plan.cols - plan.pix - RIM - width)
        low = jnp.where(after, 0, jnp.maximum(0, -first))
        high = jnp.where(after, jnp.minimum(RIM, width - first), span)
        low = jnp.where(after, low, jnp.maximum(low, span - RIM))
        tiles = blank()
        place(tiles, 0, first, low, high)
        place(tiles, 1, first, low, high, jnp.where(after, RIM, -RIM))
        put(r, plan.halves * 2 * PART, tiles)


def group_sum(x, pix):
    step = LANES // 2
    while step >= pix:
        x = x + pltpu.roll(x, step, 1)
        step //= 2
    return x


def link_kernel(plan, slot, *refs):
    n_date, own, pix = plan.n_date, plan.own, plan.pix
    groups, blocks, per, span = plan.groups, plan.blocks, plan.per, plan.span
    last = slot == plan.halves - 1
    main, days_ref, refs = refs[:n_date], refs[n_date], refs[n_date + 1 :]
    edge_ref = before_ref = None
    if last:
        edge_ref, refs = refs[0], refs[1:]
        if slot:
            before_ref, refs = refs[0], refs[1:]
    outs, refs = refs[: n_date if last else 1], refs[n_date if last else 1 :]
    (s_ref, left_ref, high_ref, low_ref, a_ref, raw_ref, cr_ref, ci_ref, ca_ref,
     mr_ref, mi_ref, ms_ref, y_ref, v_ref, ty_ref, tv_ref, a2_ref, raw2_ref) = refs
    me = lax.axis_index("date")
    chunk = plan.chunk(me)
    nt = (((1,), (1,)), ((), ()))
    rows = [slice(b, b + 40) for b in range(0, DATES, 40)]
    sub = lax.broadcasted_iota(jnp.int32, (groups, LANES), 0)
    lane = lax.broadcasted_iota(jnp.int32, (groups, LANES), 1)
    diag = jnp.where(lane // pix == sub, 1.0, 0.0).astype(f32)

    column = lax.broadcasted_iota(jnp.int32, (16, PART), 1)
    for _line in range(1, LINES):
        column = jnp.where(column >= span, column - span, column)
    spot = lax.broadcasted_iota(jnp.int32, (16, PART), 1)
    offset = column - lax.rem(lax.broadcasted_iota(jnp.int32, (16, PART), 0), pix)
    inside = (offset >= 0) & (offset <= 2 * RIM) & (spot < LINES * span)
    inside = jnp.where(inside, 1.0, 0.0).astype(f32)
    mask = jnp.concatenate([inside, inside], axis=1).astype(bf16)
    rep = jnp.concatenate([inside] * (LANES // 16), axis=0).astype(bf16)

    def to_rows(y):
        return [
            jnp.sum(y[b * groups : (b + 1) * groups] * diag, axis=0, keepdims=True) for b in range(blocks)
        ]

    for r in range(n_date):
        s_ref[r * own : (r + 1) * own, :] = main[r][:, slot * 2 * PART : (slot + 1) * 2 * PART].astype(f32)
    if last:
        is_left = chunk <= plan.left[-1]

        @pl.when(is_left | (chunk >= plan.right[-1]))
        def _():
            got = edge_ref[...].astype(f32)
            at = lax.broadcasted_iota(jnp.int32, (1, PART), 1)
            col = at
            for _line in range(1, LINES):
                col = jnp.where(col >= span, col - span, col)
            start = jnp.where(is_left, 0, span - RIM)
            valid = (col >= start) & (col < start + RIM) & (at < LINES * span)
            s_ref[:, 0:PART] = jnp.where(valid, s_ref[:, 0:PART] + got, s_ref[:, 0:PART])
            got = pltpu.roll(got, jnp.where(is_left, PART - RIM, RIM), 1)
            s_ref[:, PART : 2 * PART] = jnp.where(valid, s_ref[:, PART : 2 * PART] + got, s_ref[:, PART : 2 * PART])

    sub8 = lax.broadcasted_iota(jnp.int32, (8, LANES), 0)
    for b in range(0, DATES, 8):
        days = jnp.zeros((8, LANES), f32)
        for t in range(8):
            r, at = divmod(b + t, own)
            day = days_ref[lax.rem(me + n_date - r, n_date) * own + at].astype(f32)
            days = jnp.where(sub8 == t, day, days)
        ty_ref[0, b : b + 8] = jnp.exp(days * (1.0 / taper_days))
        ty_ref[1, b : b + 8] = jnp.exp(days * (-1.0 / taper_days))
    sr, si = s_ref[:, 0:PART], s_ref[:, PART : 2 * PART]
    left_ref[0:DATES, 0:PART] = sr.astype(bf16)
    left_ref[0:DATES, PART : 2 * PART] = si.astype(bf16)
    left_ref[DATES : 2 * DATES, 0:PART] = si.astype(bf16)
    left_ref[DATES : 2 * DATES, PART : 2 * PART] = (-sr).astype(bf16)
    left_ref[:, 2 * PART :] = left_ref[:, : 2 * PART]
    intensity = sr * sr + si * si
    weight = 1.0 / (jnp.sum(intensity, axis=0, keepdims=True) / DATES + epsilon)
    for part, s in enumerate((sr, si)):
        at = slice(part * PART, (part + 1) * PART)
        scaled = s * weight
        high = scaled.astype(bf16).astype(f32)
        high_ref[:, at] = high
        low_ref[:, at] = scaled - high
    weighted = intensity * weight
    high = weighted.astype(bf16)
    low = (weighted - high.astype(f32)).astype(bf16)
    power = lax.dot_general(high, rep, nt, preferred_element_type=f32)
    power = power + lax.dot_general(low, rep, nt, preferred_element_type=f32)
    root = lax.rsqrt(power + epsilon)
    for k in range(2):
        y = ty_ref[k] * root
        ty_ref[k] = y
        for b, row in enumerate(to_rows(y)):
            tv_ref[k, b : b + 1, :] = row

    unit = max(1, 16 // pix)

    def build(first, a_ref):
        for p in range(per):
            for g in range(0, groups, unit):
                for k, ref in enumerate((high_ref, low_ref)):
                    rows16 = jnp.concatenate(
                        [
                            jnp.broadcast_to(ref[pl.ds((first + p) * groups + g + u, 1), :], (pix, 2 * PART))
                            for u in range(unit)
                        ],
                        axis=0,
                    )
                    at = p * LANES + g * pix
                    a_ref[at : at + 16, k * 2 * PART : (k + 1) * 2 * PART] = rows16.astype(bf16) * mask

    def multiply(a_ref, raw_ref):
        raw_ref[...] = lax.dot_general(left_ref[...], a_ref[...], nt, preferred_element_type=f32)

    def normalise(first, raw_ref):
        for p in range(per):
            b = first + p
            grow_row = tv_ref[0, pl.ds(b, 1), :]
            decay_row = tv_ref[1, pl.ds(b, 1), :]
            at = slice(p * LANES, (p + 1) * LANES)
            sum_r = jnp.zeros((8, LANES), f32)
            sum_i = jnp.zeros((8, LANES), f32)
            for part in rows:
                shifted = slice(part.start + DATES, part.stop + DATES)
                factor = jnp.minimum(ty_ref[0, part] * decay_row, ty_ref[1, part] * grow_row)
                cr = raw_ref[part, at] * factor
                ci = raw_ref[shifted, at] * factor
                square = cr * cr + ci * ci
                cr_ref[b, part, :] = cr
                ci_ref[b, part, :] = ci
                ca_ref[b, part, :] = square * lax.rsqrt(jnp.maximum(square, 1e-36))
                sum_r = sum_r + jnp.sum(cr.reshape(5, 8, LANES), axis=0)
                sum_i = sum_i + jnp.sum(ci.reshape(5, 8, LANES), axis=0)
            at = pl.ds(pl.multiple_of(b * groups, groups), groups)
            y_ref[0, at] = jnp.sum(sum_r, axis=0, keepdims=True) * diag
            y_ref[1, at] = -jnp.sum(sum_i, axis=0, keepdims=True) * diag


    steps = blocks // per

    def coherence(pair, carry):
        step = 2 * pair
        multiply(a2_ref, raw2_ref)
        build((step + 2) * per, a_ref)
        normalise(step * per, raw_ref)
        multiply(a_ref, raw_ref)
        build(jnp.minimum(step + 3, steps - 1) * per, a2_ref)
        normalise((step + 1) * per, raw2_ref)
        return carry

    build(0, a_ref)
    multiply(a_ref, raw_ref)
    build(per, a2_ref)
    lax.fori_loop(0, (steps - 1) // 2, coherence, 0)
    if steps % 2 == 0:
        multiply(a2_ref, raw2_ref)
        normalise((steps - 2) * per, raw_ref)
        normalise((steps - 1) * per, raw2_ref)
    else:
        normalise((steps - 1) * per, raw_ref)

    def unit_vector(scale):
        yr = group_sum(y_ref[0], pix) * scale
        yi = group_sum(y_ref[1], pix) * scale
        mean = jnp.sum(yr * yr + yi * yi, axis=0, keepdims=True) / DATES
        inv = lax.rsqrt(mean + epsilon)
        y_ref[0] = yr * inv
        y_ref[1] = yi * inv

    def first_step():
        yr, yi = y_ref[0], y_ref[1]
        square = yr * yr + yi * yi
        y_ref[2] = square * lax.rsqrt(jnp.maximum(square, 1e-36))
        for k in range(3):
            for b, row in enumerate(to_rows(y_ref[k])):
                v_ref[k, b : b + 1, :] = row

        def body(b, carry):
            la = v_ref[2, pl.ds(b, 1), :] * reweight_gain
            lr4 = v_ref[0, pl.ds(b, 1), :] * reweight_gain
            li4 = v_ref[1, pl.ds(b, 1), :] * reweight_gain
            sum_r = jnp.zeros((8, LANES), f32)
            sum_i = jnp.zeros((8, LANES), f32)
            for part in rows:
                cr, ci = cr_ref[b, part, :], ci_ref[b, part, :]
                yr, yi = y_ref[0, part], y_ref[1, part]
                pr = cr * yr + ci * yi
                pi = cr * yi - ci * yr
                den = (1.0 + ca_ref[b, part, :] * (y_ref[2, part] * la)) - (lr4 * pr + li4 * pi)
                g = 1.0 / den
                mr, mi = cr * g, ci * g
                mr_ref[b, part, :] = mr
                mi_ref[b, part, :] = mi
                ms_ref[b, part, :] = mr + mi
                sum_r = sum_r + jnp.sum((pr * g).reshape(5, 8, LANES), axis=0)
                sum_i = sum_i + jnp.sum((pi * g).reshape(5, 8, LANES), axis=0)
            set_row(b, jnp.sum(sum_r, axis=0, keepdims=True), jnp.sum(sum_i, axis=0, keepdims=True))
            return carry

        lax.fori_loop(0, blocks, body, 0, unroll=4 if blocks % 4 == 0 else 2)

    def set_row(b, vr, vi):
        tv_ref[0, pl.ds(b, 1), :] = vr
        tv_ref[1, pl.ds(b, 1), :] = vi

    def rows_to_lanes():
        vr, vi = tv_ref[0], tv_ref[1]
        v_ref[0] = vr
        v_ref[1] = vi - vr
        v_ref[2] = vr + vi
        for part in rows:
            zero = jnp.zeros((40, LANES), f32)

            def body(b, acc, part=part):
                v0, v1, v2 = (v_ref[k, pl.ds(b, 1), :] for k in range(3))
                return (
                    acc[0] + ms_ref[b, part, :] * v0,
                    acc[1] + mr_ref[b, part, :] * v1,
                    acc[2] + mi_ref[b, part, :] * v2,
                )

            k1, k2, k3 = lax.fori_loop(0, blocks, body, (zero, zero, zero), unroll=10)
            y_ref[0, part] = k1 - k3
            y_ref[1, part] = k1 + k2

    def lanes_to_rows():
        yr = group_sum(y_ref[0], pix)
        yi = group_sum(y_ref[1], pix)
        y_ref[0] = yr
        y_ref[1] = yi - yr
        y_ref[2] = yr + yi

        def body(step, carry):
            sums = [[jnp.zeros((8, LANES), f32) for _ in range(3)] for _ in range(per)]
            for part in rows:
                y0, y1, y2 = (y_ref[k, part] for k in range(3))
                for p in range(per):
                    b = step * per + p
                    for k, (m, y) in enumerate(((ms_ref, y0), (mi_ref, y1), (mr_ref, y2))):
                        sums[p][k] += jnp.sum((m[b, part, :] * y).reshape(5, 8, LANES), axis=0)
            for p in range(per):
                k1, k2, k3 = (jnp.sum(s, axis=0, keepdims=True) for s in sums[p])
                set_row(step * per + p, k1 + k2, k3 - k1)
            return carry

        lax.fori_loop(0, blocks // per, body, 0, unroll=2 if blocks // per % 2 == 0 else 1)

    unit_vector(1.0)
    for outer in range(ITERS):
        first_step()
        for step in range(1, POWER):
            if step % 2:
                rows_to_lanes()
            else:
                lanes_to_rows()
        unit_vector(1.0 / math.sqrt(DATES) ** POWER)

    if not last:
        outs[0][...] = y_ref[0:2]
        return
    place = lax.rem(lax.broadcasted_iota(jnp.int32, (1, LANES), 1) // pix, plan.halves)
    here = place == plan.half(chunk, slot)
    for r in range(n_date):
        at = slice(r * own, (r + 1) * own)
        for k in range(2):
            value = y_ref[k, at]
            if slot:
                value = jnp.where(here, value, before_ref[k, at])
            outs[r][k] = value


def link(plan, slot, main, days, *more):
    last = slot == plan.halves - 1
    matrix = pltpu.VMEM((plan.blocks, DATES, LANES), f32)
    samples = pltpu.VMEM((DATES, 2 * PART), f32)
    if last:
        shapes = [jax.ShapeDtypeStruct((2, plan.own, LANES), f32)] * plan.n_date
    else:
        shapes = [jax.ShapeDtypeStruct((2, DATES, LANES), f32)]
    return pl.pallas_call(
        functools.partial(link_kernel, plan, slot),
        out_shape=shapes,
        in_specs=[VMEM] * plan.n_date + [pl.BlockSpec(memory_space=pltpu.SMEM)] + [VMEM] * len(more),
        out_specs=[VMEM] * len(shapes),
        scratch_shapes=[
            samples,
            pltpu.VMEM((2 * DATES, 4 * PART), bf16),
            samples,
            samples,
            pltpu.VMEM((plan.per * LANES, 4 * PART), bf16),
            pltpu.VMEM((2 * DATES, PART), f32),
        ]
        + [matrix] * 6
        + [
            pltpu.VMEM((3, DATES, LANES), f32),
            pltpu.VMEM((3, plan.blocks, LANES), f32),
            pltpu.VMEM((2, DATES, LANES), f32),
            pltpu.VMEM((2, plan.blocks, LANES), f32),
            pltpu.VMEM((plan.per * LANES, 4 * PART), bf16),
            pltpu.VMEM((2 * DATES, PART), f32),
        ],
        compiler_params=pltpu.CompilerParams(vmem_limit_bytes=24 * 2**20),
    )(*main, days, *more)


def local(acquisitions, acquisition_day):
    n_date, n_space = lax.axis_size("date"), lax.axis_size("space")
    plan = Plan(acquisitions.shape, n_date)
    own = plan.own
    me = lax.axis_index("date")

    main = pl.pallas_call(
        functools.partial(pack_kernel, plan),
        out_shape=[jax.ShapeDtypeStruct((own, plan.message), bf16)] * n_date,
        in_specs=[VMEM],
        out_specs=[VMEM] * n_date,
        scratch_shapes=[pltpu.VMEM((2, LINES, own, LANES), f32)],
        compiler_params=pltpu.CompilerParams(vmem_limit_bytes=24 * 2**20),
    )(jnp.transpose(acquisitions, (0, 2, 1, 3)))
    main = list(main)
    for r in range(1, n_date):
        main[r] = lax.ppermute(main[r], "date", [(i, (i + r) % n_date) for i in range(n_date)])
    swap = []
    for s in range(n_space - 1):
        for d in plan.right if s % 2 == 0 else plan.left:
            before, after = s * n_date + d, (s + 1) * n_date + d
            swap += [(before, after), (after, before)]
    edge = jnp.concatenate([m[:, plan.halves * 2 * PART :] for m in main], axis=0)
    edge = lax.ppermute(edge, ("space", "date"), swap)

    if plan.halves == 1:
        out = link(plan, 0, main, acquisition_day, edge)
    else:
        (before,) = link(plan, 0, main, acquisition_day)
        out = link(plan, 1, main, acquisition_day, edge, before)

    lane_owner = jnp.arange(LANES) // plan.cols
    result = out[0]
    for r in range(1, n_date):
        piece = lax.ppermute(out[r], "date", [(i, (i - r) % n_date) for i in range(n_date)])
        result = jnp.where(lane_owner == plan.chunk(lax.rem(me + r, n_date)), piece, result)
    return result


def solution(mesh):
    return jax.shard_map(
        local,
        mesh=mesh,
        in_specs=(P(None, "date", None, "space"), P()),
        out_specs=P(None, "date", "space"),
        check_vma=False,
    )
```

```python
import functools
import math

import jax
import jax.numpy as jnp
from jax import lax
from jax.experimental import pallas as pl
from jax.experimental.pallas import tpu as pltpu
from jax.sharding import PartitionSpec as P

DATES = 160
RIM = 10
LINES = 7
ITERS = 2
POWER = 4
LANES = 128
PART = 256

epsilon = 1e-06
reweight_gain = 4.0
taper_days = 360.0

f32 = jnp.float32
bf16 = jnp.bfloat16
VMEM = pl.BlockSpec(memory_space=pltpu.VMEM)


class Plan:
    def __init__(self, shape, n_date):
        self.n_date = n_date
        self.own = shape[1]
        self.width = shape[3]
        self.cols = self.width // n_date
        self.pix = min(16, self.cols)
        self.halves = self.cols // self.pix
        assert self.halves <= 2
        self.groups = LANES // self.pix
        self.blocks = DATES // self.groups
        self.per = 2 if self.blocks % 2 == 0 else 1
        self.span = self.pix + 2 * RIM
        self.left = [d for d in range(n_date) if d * self.cols < RIM]
        self.right = [n_date - 1 - d for d in self.left]
        if self.halves == 2:
            self.pieces = [(0, self.pix), (LINES * self.pix, 2 * RIM), (PART, self.pix)]
            self.tail, self.stride = PART, PART + LANES
        else:
            self.pieces = [(0, self.span)]
            self.tail, self.stride = 0, PART
        self.tail_width = self.pieces[-1][1]
        self.tail_lanes = self.stride - self.tail

    def chunk(self, date):
        odd = lax.rem(lax.axis_index("space"), 2) == 1
        return jnp.where(odd, self.n_date - 1 - date, date)

    def swapped(self, chunk):
        return chunk <= self.left[-1]

    def half(self, chunk, slot):
        if self.halves == 1:
            return 0
        return jnp.where(self.swapped(chunk), 1 - slot, slot)


def pack_kernel(plan, x_ref, *refs):
    n_date, width = plan.n_date, plan.width
    main, plane = refs[:n_date], refs[n_date]
    me = lax.axis_index("date")
    plane[...] = x_ref[...].astype(f32)
    lane = lax.broadcasted_iota(jnp.int32, (1, LANES), 1)
    tile_count = plan.stride // LANES

    def place(tiles, part, base, wide, first, low, high):
        for line in range(LINES):
            start = base + line * wide
            moved = pltpu.roll(plane[part, line], lax.rem(start - first + 8 * LANES, LANES), 1)
            for tile in range(tile_count):
                if start < (tile + 1) * LANES and start + wide > tile * LANES:
                    at = lane + (tile * LANES - start)
                    tiles[tile] = jnp.where((at >= low) & (at < high), moved, tiles[tile])

    for r in range(n_date):
        chunk = plan.chunk(lax.rem(me + r, n_date))
        swapped = plan.swapped(chunk)
        window = chunk * plan.cols - RIM
        far = window + plan.span
        for part in range(2):
            tiles = [jnp.zeros((plan.own, LANES), f32) for _ in range(tile_count)]
            for k, (base, wide) in enumerate(plan.pieces):
                if len(plan.pieces) == 1:
                    first = window
                elif k == 1:
                    first = window + plan.pix
                else:
                    first = jnp.where(swapped == (k == 2), window, far)
                low, high = jnp.maximum(0, -first), jnp.minimum(wide, width - first)
                place(tiles, part, base, wide, first, low, high)
            base, wide = plan.pieces[-1]
            place(
                tiles,
                part,
                base,
                wide,
                jnp.where(swapped, 0, width - wide),
                jnp.where(swapped, 0, jnp.minimum(wide, width - first)),
                jnp.where(swapped, -first, wide),
            )
            for k, tile in enumerate(tiles):
                at = part * plan.stride + k * LANES
                main[r][:, at : at + LANES] = tile.astype(bf16)


def unpack_kernel(plan, *refs):
    n_date, own = plan.n_date, plan.own
    pieces, out_ref = refs[:n_date], refs[n_date]
    me = lax.axis_index("date")
    region = LANES // 4
    owner = lax.broadcasted_iota(jnp.int32, (1, LANES), 1) // plan.cols
    for quarter in range(4):
        value = jnp.zeros((own // 2, LANES), f32)
        for r in range(n_date):
            chunk = plan.chunk(lax.rem(me + r, n_date))
            shift = lax.rem(chunk * plan.cols // region + 4 - quarter, 4) * region
            value = jnp.where(owner == chunk, pltpu.roll(pieces[r][...], shift, 1), value)
        start = quarter % 2 * (own // 2)
        out_ref[quarter // 2, start : start + own // 2, :] = value


def group_sum(x, pix):
    step = LANES // 2
    while step >= pix:
        x = x + pltpu.roll(x, step, 1)
        step //= 2
    return x


def link_kernel(plan, slot, *refs):
    n_date, own, pix = plan.n_date, plan.own, plan.pix
    groups, blocks, per, span = plan.groups, plan.blocks, plan.per, plan.span
    last = slot == plan.halves - 1
    main, days_ref, refs = refs[:n_date], refs[n_date], refs[n_date + 1 :]
    edge_ref = before_ref = None
    if last:
        edge_ref, refs = refs[0], refs[1:]
        if slot:
            before_ref, refs = refs[0], refs[1:]
    outs, refs = refs[: n_date if last else 1], refs[n_date if last else 1 :]
    (s_ref, left_ref, high_ref, low_ref, a_ref, raw_ref, cr_ref, ci_ref, ca_ref,
     mr_ref, mi_ref, ms_ref, y_ref, v_ref, ty_ref, tv_ref, a2_ref, raw2_ref) = refs
    me = lax.axis_index("date")
    chunk = plan.chunk(me)
    nt = (((1,), (1,)), ((), ()))
    rows = [slice(b, b + 40) for b in range(0, DATES, 40)]
    sub = lax.broadcasted_iota(jnp.int32, (groups, LANES), 0)
    lane = lax.broadcasted_iota(jnp.int32, (groups, LANES), 1)
    diag = jnp.where(lane // pix == sub, 1.0, 0.0).astype(f32)

    spot = lax.broadcasted_iota(jnp.int32, (16, PART), 1)
    if plan.halves == 1:
        layout = [(0, span, 0)]
    elif last:
        layout = [(0, 2 * RIM, plan.pix), (plan.tail - plan.pieces[1][0], pix, jnp.where(plan.swapped(chunk), 0, span))]
    else:
        layout = [(0, pix, jnp.where(plan.swapped(chunk), span, 0)), (plan.pieces[1][0], 2 * RIM, plan.pix)]
    column = jnp.full((16, PART), -LANES, jnp.int32)
    for base, wide, col in layout:
        for line in range(LINES):
            start = base + line * wide
            column = jnp.where((spot >= start) & (spot < start + wide), spot - start + col, column)
    column = column - plan.half(chunk, slot) * pix
    offset = column - lax.rem(lax.broadcasted_iota(jnp.int32, (16, PART), 0), pix)
    inside = jnp.where((offset >= 0) & (offset <= 2 * RIM), 1.0, 0.0).astype(f32)
    mask = jnp.concatenate([inside, inside], axis=1).astype(bf16)
    rep = jnp.concatenate([inside] * (LANES // 16), axis=0).astype(bf16)

    def to_rows(y):
        return [
            jnp.sum(y[b * groups : (b + 1) * groups] * diag, axis=0, keepdims=True) for b in range(blocks)
        ]

    for r in range(n_date):
        for part in range(2):
            s = main[r][:, part * plan.stride : (part + 1) * plan.stride].astype(f32)
            if slot:
                s = pltpu.roll(s, plan.stride - plan.pieces[1][0], 1)
            s_ref[r * own : (r + 1) * own, part * PART : (part + 1) * PART] = s[:, 0:PART]
    if last:
        is_left = plan.swapped(chunk)
        depth = jnp.where(is_left, chunk, n_date - 1 - chunk)
        missing = RIM - depth * plan.cols
        wide = plan.tail_width
        base = plan.tail - plan.pieces[1][0] if plan.halves == 2 else 0

        @pl.when(missing > 0)
        def _():
            at = lax.broadcasted_iota(jnp.int32, (1, PART), 1) - base
            col = at
            for _line in range(1, LINES):
                col = jnp.where(col >= wide, col - wide, col)
            low = jnp.where(is_left, 0, wide - missing)
            valid = (col >= low) & (col < low + missing) & (at >= 0) & (at < LINES * wide)
            shift = jnp.where(is_left, missing - wide, wide - missing) + base
            for part in range(2):
                got = edge_ref[:, part * plan.tail_lanes : (part + 1) * plan.tail_lanes].astype(f32)
                if plan.tail_lanes < PART:
                    got = jnp.concatenate([got, jnp.zeros((DATES, PART - plan.tail_lanes), f32)], axis=1)
                got = pltpu.roll(got, lax.rem(shift + PART, PART), 1)
                at_part = slice(part * PART, (part + 1) * PART)
                s_ref[:, at_part] = jnp.where(valid, got, s_ref[:, at_part])

    sub8 = lax.broadcasted_iota(jnp.int32, (8, LANES), 0)
    for b in range(0, DATES, 8):
        days = jnp.zeros((8, LANES), f32)
        for t in range(8):
            r, at = divmod(b + t, own)
            day = days_ref[lax.rem(me + n_date - r, n_date) * own + at].astype(f32)
            days = jnp.where(sub8 == t, day, days)
        ty_ref[0, b : b + 8] = jnp.exp(days * (1.0 / taper_days))
        ty_ref[1, b : b + 8] = jnp.exp(days * (-1.0 / taper_days))
    sr, si = s_ref[:, 0:PART], s_ref[:, PART : 2 * PART]
    left_ref[0:DATES, 0:PART] = sr.astype(bf16)
    left_ref[0:DATES, PART : 2 * PART] = si.astype(bf16)
    left_ref[DATES : 2 * DATES, 0:PART] = si.astype(bf16)
    left_ref[DATES : 2 * DATES, PART : 2 * PART] = (-sr).astype(bf16)
    left_ref[:, 2 * PART :] = left_ref[:, : 2 * PART]
    intensity = sr * sr + si * si
    weight = 1.0 / (jnp.sum(intensity, axis=0, keepdims=True) / DATES + epsilon)
    for part, s in enumerate((sr, si)):
        at = slice(part * PART, (part + 1) * PART)
        scaled = s * weight
        high = scaled.astype(bf16).astype(f32)
        high_ref[:, at] = high
        low_ref[:, at] = scaled - high
    weighted = intensity * weight
    high = weighted.astype(bf16)
    low = (weighted - high.astype(f32)).astype(bf16)
    power = lax.dot_general(high, rep, nt, preferred_element_type=f32)
    power = power + lax.dot_general(low, rep, nt, preferred_element_type=f32)
    root = lax.rsqrt(power + epsilon)
    for k in range(2):
        y = ty_ref[k] * root
        ty_ref[k] = y
        for b, row in enumerate(to_rows(y)):
            tv_ref[k, b : b + 1, :] = row

    unit = max(1, 16 // pix)

    def build(first, a_ref):
        for p in range(per):
            for g in range(0, groups, unit):
                for k, ref in enumerate((high_ref, low_ref)):
                    rows16 = jnp.concatenate(
                        [
                            jnp.broadcast_to(ref[pl.ds((first + p) * groups + g + u, 1), :], (pix, 2 * PART))
                            for u in range(unit)
                        ],
                        axis=0,
                    )
                    at = p * LANES + g * pix
                    a_ref[at : at + 16, k * 2 * PART : (k + 1) * 2 * PART] = rows16.astype(bf16) * mask

    def multiply(a_ref, raw_ref):
        raw_ref[...] = lax.dot_general(left_ref[...], a_ref[...], nt, preferred_element_type=f32)

    def normalise(first, raw_ref):
        for p in range(per):
            b = first + p
            grow_row = tv_ref[0, pl.ds(b, 1), :]
            decay_row = tv_ref[1, pl.ds(b, 1), :]
            at = slice(p * LANES, (p + 1) * LANES)
            sum_r = jnp.zeros((8, LANES), f32)
            sum_i = jnp.zeros((8, LANES), f32)
            for part in rows:
                shifted = slice(part.start + DATES, part.stop + DATES)
                factor = jnp.minimum(ty_ref[0, part] * decay_row, ty_ref[1, part] * grow_row)
                cr = raw_ref[part, at] * factor
                ci = raw_ref[shifted, at] * factor
                square = cr * cr + ci * ci
                cr_ref[b, part, :] = cr
                ci_ref[b, part, :] = ci
                ca_ref[b, part, :] = square * lax.rsqrt(jnp.maximum(square, 1e-36))
                sum_r = sum_r + jnp.sum(cr.reshape(5, 8, LANES), axis=0)
                sum_i = sum_i + jnp.sum(ci.reshape(5, 8, LANES), axis=0)
            at = pl.ds(pl.multiple_of(b * groups, groups), groups)
            y_ref[0, at] = jnp.sum(sum_r, axis=0, keepdims=True) * diag
            y_ref[1, at] = -jnp.sum(sum_i, axis=0, keepdims=True) * diag


    steps = blocks // per

    def coherence(pair, carry):
        step = 2 * pair
        multiply(a2_ref, raw2_ref)
        build((step + 2) * per, a_ref)
        normalise(step * per, raw_ref)
        multiply(a_ref, raw_ref)
        build(jnp.minimum(step + 3, steps - 1) * per, a2_ref)
        normalise((step + 1) * per, raw2_ref)
        return carry

    build(0, a_ref)
    multiply(a_ref, raw_ref)
    build(per, a2_ref)
    lax.fori_loop(0, (steps - 1) // 2, coherence, 0)
    if steps % 2 == 0:
        multiply(a2_ref, raw2_ref)
        normalise((steps - 2) * per, raw_ref)
        normalise((steps - 1) * per, raw2_ref)
    else:
        normalise((steps - 1) * per, raw_ref)

    def unit_vector(scale):
        yr = group_sum(y_ref[0], pix) * scale
        yi = group_sum(y_ref[1], pix) * scale
        mean = jnp.sum(yr * yr + yi * yi, axis=0, keepdims=True) / DATES
        inv = lax.rsqrt(mean + epsilon)
        y_ref[0] = yr * inv
        y_ref[1] = yi * inv

    def first_step():
        yr, yi = y_ref[0], y_ref[1]
        square = yr * yr + yi * yi
        y_ref[2] = square * lax.rsqrt(jnp.maximum(square, 1e-36))
        for k in range(3):
            for b, row in enumerate(to_rows(y_ref[k])):
                v_ref[k, b : b + 1, :] = row

        def body(b, carry):
            la = v_ref[2, pl.ds(b, 1), :] * reweight_gain
            lr4 = v_ref[0, pl.ds(b, 1), :] * reweight_gain
            li4 = v_ref[1, pl.ds(b, 1), :] * reweight_gain
            sum_r = jnp.zeros((8, LANES), f32)
            sum_i = jnp.zeros((8, LANES), f32)
            for part in rows:
                cr, ci = cr_ref[b, part, :], ci_ref[b, part, :]
                yr, yi = y_ref[0, part], y_ref[1, part]
                pr = cr * yr + ci * yi
                pi = cr * yi - ci * yr
                den = (1.0 + ca_ref[b, part, :] * (y_ref[2, part] * la)) - (lr4 * pr + li4 * pi)
                g = 1.0 / den
                mr, mi = cr * g, ci * g
                mr_ref[b, part, :] = mr
                mi_ref[b, part, :] = mi
                ms_ref[b, part, :] = mr + mi
                sum_r = sum_r + jnp.sum((pr * g).reshape(5, 8, LANES), axis=0)
                sum_i = sum_i + jnp.sum((pi * g).reshape(5, 8, LANES), axis=0)
            set_row(b, jnp.sum(sum_r, axis=0, keepdims=True), jnp.sum(sum_i, axis=0, keepdims=True))
            return carry

        lax.fori_loop(0, blocks, body, 0, unroll=4 if blocks % 4 == 0 else 2)

    def set_row(b, vr, vi):
        tv_ref[0, pl.ds(b, 1), :] = vr
        tv_ref[1, pl.ds(b, 1), :] = vi

    def rows_to_lanes():
        vr, vi = tv_ref[0], tv_ref[1]
        v_ref[0] = vr
        v_ref[1] = vi - vr
        v_ref[2] = vr + vi
        for part in rows:
            zero = jnp.zeros((40, LANES), f32)

            def body(b, acc, part=part):
                v0, v1, v2 = (v_ref[k, pl.ds(b, 1), :] for k in range(3))
                return (
                    acc[0] + ms_ref[b, part, :] * v0,
                    acc[1] + mr_ref[b, part, :] * v1,
                    acc[2] + mi_ref[b, part, :] * v2,
                )

            k1, k2, k3 = lax.fori_loop(0, blocks, body, (zero, zero, zero), unroll=10)
            y_ref[0, part] = k1 - k3
            y_ref[1, part] = k1 + k2

    def lanes_to_rows():
        yr = group_sum(y_ref[0], pix)
        yi = group_sum(y_ref[1], pix)
        y_ref[0] = yr
        y_ref[1] = yi - yr
        y_ref[2] = yr + yi

        def body(step, carry):
            sums = [[jnp.zeros((8, LANES), f32) for _ in range(3)] for _ in range(per)]
            for part in rows:
                y0, y1, y2 = (y_ref[k, part] for k in range(3))
                for p in range(per):
                    b = step * per + p
                    for k, (m, y) in enumerate(((ms_ref, y0), (mi_ref, y1), (mr_ref, y2))):
                        sums[p][k] += jnp.sum((m[b, part, :] * y).reshape(5, 8, LANES), axis=0)
            for p in range(per):
                k1, k2, k3 = (jnp.sum(s, axis=0, keepdims=True) for s in sums[p])
                set_row(step * per + p, k1 + k2, k3 - k1)
            return carry

        lax.fori_loop(0, blocks // per, body, 0, unroll=2 if blocks // per % 2 == 0 else 1)

    unit_vector(1.0)
    for outer in range(ITERS):
        first_step()
        for step in range(1, POWER):
            if step % 2:
                rows_to_lanes()
            else:
                lanes_to_rows()
        unit_vector(1.0 / math.sqrt(DATES) ** POWER)

    if not last:
        outs[0][...] = y_ref[0:2]
        return
    lane_row = lax.broadcasted_iota(jnp.int32, (1, LANES), 1)
    here = lax.rem(lane_row // pix, plan.halves) == plan.half(chunk, slot)
    quarter = lane_row // (LANES // 4)
    for r in range(n_date):
        value = None
        for q in range(4):
            start = r * own + q % 2 * (own // 2)
            at = slice(start, start + own // 2)
            piece = y_ref[q // 2, at]
            if slot:
                piece = jnp.where(here, piece, before_ref[q // 2, at])
            value = piece if value is None else jnp.where(quarter == q, piece, value)
        outs[r][...] = value


def link(plan, slot, main, days, *more):
    last = slot == plan.halves - 1
    matrix = pltpu.VMEM((plan.blocks, DATES, LANES), f32)
    samples = pltpu.VMEM((DATES, 2 * PART), f32)
    if last:
        shapes = [jax.ShapeDtypeStruct((plan.own // 2, LANES), f32)] * plan.n_date
    else:
        shapes = [jax.ShapeDtypeStruct((2, DATES, LANES), f32)]
    return pl.pallas_call(
        functools.partial(link_kernel, plan, slot),
        out_shape=shapes,
        in_specs=[VMEM] * plan.n_date + [pl.BlockSpec(memory_space=pltpu.SMEM)] + [VMEM] * len(more),
        out_specs=[VMEM] * len(shapes),
        scratch_shapes=[
            samples,
            pltpu.VMEM((2 * DATES, 4 * PART), bf16),
            samples,
            samples,
            pltpu.VMEM((plan.per * LANES, 4 * PART), bf16),
            pltpu.VMEM((2 * DATES, PART), f32),
        ]
        + [matrix] * 6
        + [
            pltpu.VMEM((3, DATES, LANES), f32),
            pltpu.VMEM((3, plan.blocks, LANES), f32),
            pltpu.VMEM((2, DATES, LANES), f32),
            pltpu.VMEM((2, plan.blocks, LANES), f32),
            pltpu.VMEM((plan.per * LANES, 4 * PART), bf16),
            pltpu.VMEM((2 * DATES, PART), f32),
        ],
        compiler_params=pltpu.CompilerParams(vmem_limit_bytes=24 * 2**20),
    )(*main, days, *more)


def local(acquisitions, acquisition_day):
    n_date, n_space = lax.axis_size("date"), lax.axis_size("space")
    plan = Plan(acquisitions.shape, n_date)
    own = plan.own

    main = pl.pallas_call(
        functools.partial(pack_kernel, plan),
        out_shape=[jax.ShapeDtypeStruct((own, 2 * plan.stride), bf16)] * n_date,
        in_specs=[VMEM],
        out_specs=[VMEM] * n_date,
        scratch_shapes=[pltpu.VMEM((2, LINES, own, LANES), f32)],
        compiler_params=pltpu.CompilerParams(vmem_limit_bytes=24 * 2**20),
    )(jnp.transpose(acquisitions, (0, 2, 1, 3)))
    main = list(main)
    for r in range(1, n_date):
        main[r] = lax.ppermute(main[r], "date", [(i, (i + r) % n_date) for i in range(n_date)])
    swap = []
    for s in range(n_space - 1):
        for d in plan.right if s % 2 == 0 else plan.left:
            before, after = s * n_date + d, (s + 1) * n_date + d
            swap += [(before, after), (after, before)]
    edge = jnp.concatenate(
        [
            jnp.concatenate([m[:, k * plan.stride + plan.tail : (k + 1) * plan.stride] for k in range(2)], axis=1)
            for m in main
        ],
        axis=0,
    )
    edge = lax.ppermute(edge, ("space", "date"), swap)

    if plan.halves == 1:
        out = link(plan, 0, main, acquisition_day, edge)
    else:
        (before,) = link(plan, 0, main, acquisition_day)
        out = link(plan, 1, main, acquisition_day, edge, before)

    pieces = [out[0]]
    for r in range(1, n_date):
        pieces.append(lax.ppermute(out[r], "date", [(i, (i - r) % n_date) for i in range(n_date)]))
    return pl.pallas_call(
        functools.partial(unpack_kernel, plan),
        out_shape=jax.ShapeDtypeStruct((2, own, plan.width), f32),
        in_specs=[VMEM] * n_date,
        out_specs=VMEM,
        compiler_params=pltpu.CompilerParams(vmem_limit_bytes=24 * 2**20),
    )(*pieces)


def solution(mesh):
    return jax.shard_map(
        local,
        mesh=mesh,
        in_specs=(P(None, "date", None, "space"), P()),
        out_specs=P(None, "date", "space"),
        check_vma=False,
    )
```

```python
import functools
import math

import jax
import jax.numpy as jnp
from jax import lax
from jax.experimental import pallas as pl
from jax.experimental.pallas import tpu as pltpu
from jax.sharding import PartitionSpec as P

DATES = 160
RIM = 10
LINES = 7
ITERS = 2
POWER = 4
LANES = 128
PART = 256

epsilon = 1e-06
reweight_gain = 4.0
taper_days = 360.0

f32 = jnp.float32
bf16 = jnp.bfloat16
VMEM = pl.BlockSpec(memory_space=pltpu.VMEM)


class Plan:
    def __init__(self, shape, n_date):
        self.n_date = n_date
        self.own = shape[1]
        self.width = shape[3]
        self.cols = self.width // n_date
        self.pix = min(16, self.cols)
        self.halves = self.cols // self.pix
        assert self.halves <= 2
        self.groups = LANES // self.pix
        self.blocks = DATES // self.groups
        self.per = 2 if self.blocks % 2 == 0 else 1
        self.span = self.pix + 2 * RIM
        self.left = [d for d in range(n_date) if d * self.cols < RIM]
        self.right = [n_date - 1 - d for d in self.left]
        if self.halves == 2:
            self.pieces = [(0, self.pix), (LINES * self.pix, 2 * RIM), (PART, self.pix)]
            self.tail, self.stride = PART, PART + LANES
        else:
            self.pieces = [(0, self.span)]
            self.tail, self.stride = 0, PART
        self.tail_width = self.pieces[-1][1]
        self.tail_lanes = self.stride - self.tail

    def chunk(self, date):
        odd = lax.rem(lax.axis_index("space"), 2) == 1
        return jnp.where(odd, self.n_date - 1 - date, date)

    def swapped(self, chunk):
        return chunk <= self.left[-1]

    def half(self, chunk, slot):
        if self.halves == 1:
            return 0
        return jnp.where(self.swapped(chunk), 1 - slot, slot)


def pack_kernel(plan, x_ref, *refs):
    n_date, width = plan.n_date, plan.width
    main, plane = refs[:n_date], refs[n_date]
    me = lax.axis_index("date")
    plane[...] = x_ref[...].astype(f32)
    lane = lax.broadcasted_iota(jnp.int32, (1, LANES), 1)
    tile_count = plan.stride // LANES

    def place(tiles, part, base, wide, first, low, high):
        for line in range(LINES):
            start = base + line * wide
            moved = pltpu.roll(plane[part, line], lax.rem(start - first + 8 * LANES, LANES), 1)
            for tile in range(tile_count):
                if start < (tile + 1) * LANES and start + wide > tile * LANES:
                    at = lane + (tile * LANES - start)
                    tiles[tile] = jnp.where((at >= low) & (at < high), moved, tiles[tile])

    for r in range(n_date):
        chunk = plan.chunk(lax.rem(me + r, n_date))
        swapped = plan.swapped(chunk)
        window = chunk * plan.cols - RIM
        far = window + plan.span
        for part in range(2):
            tiles = [jnp.zeros((plan.own, LANES), f32) for _ in range(tile_count)]
            for k, (base, wide) in enumerate(plan.pieces):
                if len(plan.pieces) == 1:
                    first = window
                elif k == 1:
                    first = window + plan.pix
                else:
                    first = jnp.where(swapped == (k == 2), window, far)
                low, high = jnp.maximum(0, -first), jnp.minimum(wide, width - first)
                place(tiles, part, base, wide, first, low, high)
            base, wide = plan.pieces[-1]
            place(
                tiles,
                part,
                base,
                wide,
                jnp.where(swapped, 0, width - wide),
                jnp.where(swapped, 0, jnp.minimum(wide, width - first)),
                jnp.where(swapped, -first, wide),
            )
            for k, tile in enumerate(tiles):
                at = part * plan.stride + k * LANES
                main[r][:, at : at + LANES] = tile.astype(bf16)


def unpack_kernel(plan, *refs):
    n_date, own = plan.n_date, plan.own
    pieces, out_ref = refs[:n_date], refs[n_date]
    me = lax.axis_index("date")
    region = LANES // 4
    owner = lax.broadcasted_iota(jnp.int32, (1, LANES), 1) // plan.cols
    for quarter in range(4):
        value = jnp.zeros((own // 2, LANES), f32)
        for r in range(n_date):
            chunk = plan.chunk(lax.rem(me + r, n_date))
            shift = lax.rem(chunk * plan.cols // region + 4 - quarter, 4) * region
            value = jnp.where(owner == chunk, pltpu.roll(pieces[r][...], shift, 1), value)
        start = quarter % 2 * (own // 2)
        out_ref[quarter // 2, start : start + own // 2, :] = value


def group_sum(x, pix):
    step = LANES // 2
    while step >= pix:
        x = x + pltpu.roll(x, step, 1)
        step //= 2
    return x


def link_kernel(plan, slot, *refs):
    n_date, own, pix = plan.n_date, plan.own, plan.pix
    groups, blocks, per, span = plan.groups, plan.blocks, plan.per, plan.span
    last = slot == plan.halves - 1
    main, days_ref, refs = refs[:n_date], refs[n_date], refs[n_date + 1 :]
    edge_ref = before_ref = None
    if last:
        edge_ref, refs = refs[0], refs[1:]
        if slot:
            before_ref, refs = refs[0], refs[1:]
    outs, refs = refs[: n_date if last else 1], refs[n_date if last else 1 :]
    (s_ref, left_ref, high_ref, low_ref, a_ref, raw_ref, cr_ref, ci_ref, ca_ref,
     mr_ref, mi_ref, ms_ref, y_ref, v_ref, ty_ref, tv_ref, a2_ref, raw2_ref) = refs
    me = lax.axis_index("date")
    chunk = plan.chunk(me)
    nt = (((1,), (1,)), ((), ()))
    rows = [slice(b, b + 40) for b in range(0, DATES, 40)]
    sub = lax.broadcasted_iota(jnp.int32, (groups, LANES), 0)
    lane = lax.broadcasted_iota(jnp.int32, (groups, LANES), 1)
    diag = jnp.where(lane // pix == sub, 1.0, 0.0).astype(f32)

    spot = lax.broadcasted_iota(jnp.int32, (16, PART), 1)
    if plan.halves == 1:
        layout = [(0, span, 0)]
    elif last:
        layout = [(0, 2 * RIM, plan.pix), (plan.tail - plan.pieces[1][0], pix, jnp.where(plan.swapped(chunk), 0, span))]
    else:
        layout = [(0, pix, jnp.where(plan.swapped(chunk), span, 0)), (plan.pieces[1][0], 2 * RIM, plan.pix)]
    column = jnp.full((16, PART), -LANES, jnp.int32)
    for base, wide, col in layout:
        for line in range(LINES):
            start = base + line * wide
            column = jnp.where((spot >= start) & (spot < start + wide), spot - start + col, column)
    column = column - plan.half(chunk, slot) * pix
    offset = column - lax.rem(lax.broadcasted_iota(jnp.int32, (16, PART), 0), pix)
    inside = jnp.where((offset >= 0) & (offset <= 2 * RIM), 1.0, 0.0).astype(f32)
    mask = jnp.concatenate([inside, inside], axis=1).astype(bf16)
    rep = jnp.concatenate([inside] * (LANES // 16), axis=0).astype(bf16)

    def to_rows(y):
        return [
            jnp.sum(y[b * groups : (b + 1) * groups] * diag, axis=0, keepdims=True) for b in range(blocks)
        ]

    for r in range(n_date):
        for part in range(2):
            s = main[r][:, part * plan.stride : (part + 1) * plan.stride].astype(f32)
            if slot:
                s = pltpu.roll(s, plan.stride - plan.pieces[1][0], 1)
            s_ref[r * own : (r + 1) * own, part * PART : (part + 1) * PART] = s[:, 0:PART]
    if last:
        is_left = plan.swapped(chunk)
        depth = jnp.where(is_left, chunk, n_date - 1 - chunk)
        missing = RIM - depth * plan.cols
        wide = plan.tail_width
        base = plan.tail - plan.pieces[1][0] if plan.halves == 2 else 0

        @pl.when(missing > 0)
        def _():
            at = lax.broadcasted_iota(jnp.int32, (1, PART), 1) - base
            col = at
            for _line in range(1, LINES):
                col = jnp.where(col >= wide, col - wide, col)
            low = jnp.where(is_left, 0, wide - missing)
            valid = (col >= low) & (col < low + missing) & (at >= 0) & (at < LINES * wide)
            shift = jnp.where(is_left, missing - wide, wide - missing) + base
            for part in range(2):
                got = edge_ref[:, part * plan.tail_lanes : (part + 1) * plan.tail_lanes].astype(f32)
                if plan.tail_lanes < PART:
                    got = jnp.concatenate([got, jnp.zeros((DATES, PART - plan.tail_lanes), f32)], axis=1)
                got = pltpu.roll(got, lax.rem(shift + PART, PART), 1)
                at_part = slice(part * PART, (part + 1) * PART)
                s_ref[:, at_part] = jnp.where(valid, got, s_ref[:, at_part])

    sub8 = lax.broadcasted_iota(jnp.int32, (8, LANES), 0)
    for b in range(0, DATES, 8):
        days = jnp.zeros((8, LANES), f32)
        for t in range(8):
            r, at = divmod(b + t, own)
            day = days_ref[lax.rem(me + n_date - r, n_date) * own + at].astype(f32)
            days = jnp.where(sub8 == t, day, days)
        ty_ref[0, b : b + 8] = jnp.exp(days * (1.0 / taper_days))
        ty_ref[1, b : b + 8] = jnp.exp(days * (-1.0 / taper_days))
    sr, si = s_ref[:, 0:PART], s_ref[:, PART : 2 * PART]
    left_ref[0:DATES, 0:PART] = sr.astype(bf16)
    left_ref[0:DATES, PART : 2 * PART] = si.astype(bf16)
    left_ref[DATES : 2 * DATES, 0:PART] = si.astype(bf16)
    left_ref[DATES : 2 * DATES, PART : 2 * PART] = (-sr).astype(bf16)
    left_ref[:, 2 * PART :] = left_ref[:, : 2 * PART]
    intensity = sr * sr + si * si
    weight = 1.0 / (jnp.sum(intensity, axis=0, keepdims=True) / DATES + epsilon)
    for part, s in enumerate((sr, si)):
        at = slice(part * PART, (part + 1) * PART)
        scaled = s * weight
        high = scaled.astype(bf16).astype(f32)
        high_ref[:, at] = high
        low_ref[:, at] = scaled - high
    weighted = intensity * weight
    high = weighted.astype(bf16)
    low = (weighted - high.astype(f32)).astype(bf16)
    power = lax.dot_general(high, rep, nt, preferred_element_type=f32)
    power = power + lax.dot_general(low, rep, nt, preferred_element_type=f32)
    root = lax.rsqrt(power + epsilon)
    for k in range(2):
        y = ty_ref[k] * root
        ty_ref[k] = y
        for b, row in enumerate(to_rows(y)):
            tv_ref[k, b : b + 1, :] = row

    unit = max(1, 16 // pix)

    def build(first, a_ref):
        for p in range(per):
            for g in range(0, groups, unit):
                for k, ref in enumerate((high_ref, low_ref)):
                    rows16 = jnp.concatenate(
                        [
                            jnp.broadcast_to(ref[pl.ds((first + p) * groups + g + u, 1), :], (pix, 2 * PART))
                            for u in range(unit)
                        ],
                        axis=0,
                    )
                    at = p * LANES + g * pix
                    a_ref[at : at + 16, k * 2 * PART : (k + 1) * 2 * PART] = rows16.astype(bf16) * mask

    def multiply(a_ref, raw_ref):
        raw_ref[...] = lax.dot_general(left_ref[...], a_ref[...], nt, preferred_element_type=f32)

    def normalise(first, raw_ref):
        for p in range(per):
            b = first + p
            grow_row = tv_ref[0, pl.ds(b, 1), :]
            decay_row = tv_ref[1, pl.ds(b, 1), :]
            at = slice(p * LANES, (p + 1) * LANES)
            sum_r = jnp.zeros((8, LANES), f32)
            sum_i = jnp.zeros((8, LANES), f32)
            for part in rows:
                shifted = slice(part.start + DATES, part.stop + DATES)
                factor = jnp.minimum(ty_ref[0, part] * decay_row, ty_ref[1, part] * grow_row)
                cr = raw_ref[part, at] * factor
                ci = raw_ref[shifted, at] * factor
                square = cr * cr + ci * ci
                cr_ref[b, part, :] = cr
                ci_ref[b, part, :] = ci
                ca_ref[b, part, :] = square * lax.rsqrt(jnp.maximum(square, 1e-36))
                sum_r = sum_r + jnp.sum(cr.reshape(5, 8, LANES), axis=0)
                sum_i = sum_i + jnp.sum(ci.reshape(5, 8, LANES), axis=0)
            at = pl.ds(pl.multiple_of(b * groups, groups), groups)
            y_ref[0, at] = jnp.sum(sum_r, axis=0, keepdims=True) * diag
            y_ref[1, at] = -jnp.sum(sum_i, axis=0, keepdims=True) * diag


    steps = blocks // per

    def coherence(pair, carry):
        step = 2 * pair
        multiply(a2_ref, raw2_ref)
        build((step + 2) * per, a_ref)
        normalise(step * per, raw_ref)
        multiply(a_ref, raw_ref)
        build(jnp.minimum(step + 3, steps - 1) * per, a2_ref)
        normalise((step + 1) * per, raw2_ref)
        return carry

    build(0, a_ref)
    multiply(a_ref, raw_ref)
    build(per, a2_ref)
    for pair in range((steps - 1) // 2):
        coherence(pair, 0)
    if steps % 2 == 0:
        multiply(a2_ref, raw2_ref)
        normalise((steps - 2) * per, raw_ref)
        normalise((steps - 1) * per, raw2_ref)
    else:
        normalise((steps - 1) * per, raw_ref)

    def unit_vector(scale):
        yr = group_sum(y_ref[0], pix) * scale
        yi = group_sum(y_ref[1], pix) * scale
        mean = jnp.sum(yr * yr + yi * yi, axis=0, keepdims=True) / DATES
        inv = lax.rsqrt(mean + epsilon)
        y_ref[0] = yr * inv
        y_ref[1] = yi * inv

    def first_step():
        yr, yi = y_ref[0], y_ref[1]
        square = yr * yr + yi * yi
        y_ref[2] = square * lax.rsqrt(jnp.maximum(square, 1e-36))
        for k in range(3):
            for b, row in enumerate(to_rows(y_ref[k])):
                v_ref[k, b : b + 1, :] = row

        def body(b, carry):
            la = v_ref[2, pl.ds(b, 1), :] * reweight_gain
            lr4 = v_ref[0, pl.ds(b, 1), :] * reweight_gain
            li4 = v_ref[1, pl.ds(b, 1), :] * reweight_gain
            sum_r = jnp.zeros((8, LANES), f32)
            sum_i = jnp.zeros((8, LANES), f32)
            for part in rows:
                cr, ci = cr_ref[b, part, :], ci_ref[b, part, :]
                yr, yi = y_ref[0, part], y_ref[1, part]
                pr = cr * yr + ci * yi
                pi = cr * yi - ci * yr
                den = (1.0 + ca_ref[b, part, :] * (y_ref[2, part] * la)) - (lr4 * pr + li4 * pi)
                g = 1.0 / den
                mr, mi = cr * g, ci * g
                mr_ref[b, part, :] = mr
                mi_ref[b, part, :] = mi
                ms_ref[b, part, :] = mr + mi
                sum_r = sum_r + jnp.sum((pr * g).reshape(5, 8, LANES), axis=0)
                sum_i = sum_i + jnp.sum((pi * g).reshape(5, 8, LANES), axis=0)
            set_row(b, jnp.sum(sum_r, axis=0, keepdims=True), jnp.sum(sum_i, axis=0, keepdims=True))
            return carry

        lax.fori_loop(0, blocks, body, 0, unroll=4 if blocks % 4 == 0 else 2)

    def set_row(b, vr, vi):
        tv_ref[0, pl.ds(b, 1), :] = vr
        tv_ref[1, pl.ds(b, 1), :] = vi

    def rows_to_lanes():
        vr, vi = tv_ref[0], tv_ref[1]
        v_ref[0] = vr
        v_ref[1] = vi - vr
        v_ref[2] = vr + vi
        for part in rows:
            zero = jnp.zeros((40, LANES), f32)

            def body(b, acc, part=part):
                v0, v1, v2 = (v_ref[k, pl.ds(b, 1), :] for k in range(3))
                return (
                    acc[0] + ms_ref[b, part, :] * v0,
                    acc[1] + mr_ref[b, part, :] * v1,
                    acc[2] + mi_ref[b, part, :] * v2,
                )

            k1, k2, k3 = lax.fori_loop(0, blocks, body, (zero, zero, zero), unroll=10)
            y_ref[0, part] = k1 - k3
            y_ref[1, part] = k1 + k2

    def lanes_to_rows():
        yr = group_sum(y_ref[0], pix)
        yi = group_sum(y_ref[1], pix)
        y_ref[0] = yr
        y_ref[1] = yi - yr
        y_ref[2] = yr + yi

        def body(step, carry):
            sums = [[jnp.zeros((8, LANES), f32) for _ in range(3)] for _ in range(per)]
            for part in rows:
                y0, y1, y2 = (y_ref[k, part] for k in range(3))
                for p in range(per):
                    b = step * per + p
                    for k, (m, y) in enumerate(((ms_ref, y0), (mi_ref, y1), (mr_ref, y2))):
                        sums[p][k] += jnp.sum((m[b, part, :] * y).reshape(5, 8, LANES), axis=0)
            for p in range(per):
                k1, k2, k3 = (jnp.sum(s, axis=0, keepdims=True) for s in sums[p])
                set_row(step * per + p, k1 + k2, k3 - k1)
            return carry

        lax.fori_loop(0, blocks // per, body, 0, unroll=2 if blocks // per % 2 == 0 else 1)

    unit_vector(1.0)
    for outer in range(ITERS):
        first_step()
        for step in range(1, POWER):
            if step % 2:
                rows_to_lanes()
            else:
                lanes_to_rows()
        unit_vector(1.0 / math.sqrt(DATES) ** POWER)

    if not last:
        outs[0][...] = y_ref[0:2]
        return
    lane_row = lax.broadcasted_iota(jnp.int32, (1, LANES), 1)
    here = lax.rem(lane_row // pix, plan.halves) == plan.half(chunk, slot)
    quarter = lane_row // (LANES // 4)
    for r in range(n_date):
        value = None
        for q in range(4):
            start = r * own + q % 2 * (own // 2)
            at = slice(start, start + own // 2)
            piece = y_ref[q // 2, at]
            if slot:
                piece = jnp.where(here, piece, before_ref[q // 2, at])
            value = piece if value is None else jnp.where(quarter == q, piece, value)
        outs[r][...] = value


def link(plan, slot, main, days, *more):
    last = slot == plan.halves - 1
    matrix = pltpu.VMEM((plan.blocks, DATES, LANES), f32)
    samples = pltpu.VMEM((DATES, 2 * PART), f32)
    if last:
        shapes = [jax.ShapeDtypeStruct((plan.own // 2, LANES), f32)] * plan.n_date
    else:
        shapes = [jax.ShapeDtypeStruct((2, DATES, LANES), f32)]
    return pl.pallas_call(
        functools.partial(link_kernel, plan, slot),
        out_shape=shapes,
        in_specs=[VMEM] * plan.n_date + [pl.BlockSpec(memory_space=pltpu.SMEM)] + [VMEM] * len(more),
        out_specs=[VMEM] * len(shapes),
        scratch_shapes=[
            samples,
            pltpu.VMEM((2 * DATES, 4 * PART), bf16),
            samples,
            samples,
            pltpu.VMEM((plan.per * LANES, 4 * PART), bf16),
            pltpu.VMEM((2 * DATES, PART), f32),
        ]
        + [matrix] * 6
        + [
            pltpu.VMEM((3, DATES, LANES), f32),
            pltpu.VMEM((3, plan.blocks, LANES), f32),
            pltpu.VMEM((2, DATES, LANES), f32),
            pltpu.VMEM((2, plan.blocks, LANES), f32),
            pltpu.VMEM((plan.per * LANES, 4 * PART), bf16),
            pltpu.VMEM((2 * DATES, PART), f32),
        ],
        compiler_params=pltpu.CompilerParams(vmem_limit_bytes=24 * 2**20),
    )(*main, days, *more)


def local(acquisitions, acquisition_day):
    n_date, n_space = lax.axis_size("date"), lax.axis_size("space")
    plan = Plan(acquisitions.shape, n_date)
    own = plan.own

    main = pl.pallas_call(
        functools.partial(pack_kernel, plan),
        out_shape=[jax.ShapeDtypeStruct((own, 2 * plan.stride), bf16)] * n_date,
        in_specs=[VMEM],
        out_specs=[VMEM] * n_date,
        scratch_shapes=[pltpu.VMEM((2, LINES, own, LANES), f32)],
        compiler_params=pltpu.CompilerParams(vmem_limit_bytes=24 * 2**20),
    )(jnp.transpose(acquisitions, (0, 2, 1, 3)))
    main = list(main)
    for r in range(1, n_date):
        main[r] = lax.ppermute(main[r], "date", [(i, (i + r) % n_date) for i in range(n_date)])
    swap = []
    for s in range(n_space - 1):
        for d in plan.right if s % 2 == 0 else plan.left:
            before, after = s * n_date + d, (s + 1) * n_date + d
            swap += [(before, after), (after, before)]
    edge = jnp.concatenate(
        [
            jnp.concatenate([m[:, k * plan.stride + plan.tail : (k + 1) * plan.stride] for k in range(2)], axis=1)
            for m in main
        ],
        axis=0,
    )
    edge = lax.ppermute(edge, ("space", "date"), swap)

    if plan.halves == 1:
        out = link(plan, 0, main, acquisition_day, edge)
    else:
        (before,) = link(plan, 0, main, acquisition_day)
        out = link(plan, 1, main, acquisition_day, edge, before)

    pieces = [out[0]]
    for r in range(1, n_date):
        pieces.append(lax.ppermute(out[r], "date", [(i, (i - r) % n_date) for i in range(n_date)]))
    return pl.pallas_call(
        functools.partial(unpack_kernel, plan),
        out_shape=jax.ShapeDtypeStruct((2, own, plan.width), f32),
        in_specs=[VMEM] * n_date,
        out_specs=VMEM,
        compiler_params=pltpu.CompilerParams(vmem_limit_bytes=24 * 2**20),
    )(*pieces)


def solution(mesh):
    return jax.shard_map(
        local,
        mesh=mesh,
        in_specs=(P(None, "date", None, "space"), P()),
        out_specs=P(None, "date", "space"),
        check_vma=False,
    )
```

```python
import functools
import math

import jax
import jax.numpy as jnp
from jax import lax
from jax.experimental import pallas as pl
from jax.experimental.pallas import tpu as pltpu
from jax.sharding import PartitionSpec as P

DATES = 160
RIM = 10
LINES = 7
ITERS = 2
POWER = 4
LANES = 128
PART = 256

epsilon = 1e-06
reweight_gain = 4.0
taper_days = 360.0

f32 = jnp.float32
bf16 = jnp.bfloat16
VMEM = pl.BlockSpec(memory_space=pltpu.VMEM)


class Plan:
    def __init__(self, shape, n_date):
        self.n_date = n_date
        self.own = shape[1]
        self.width = shape[3]
        self.cols = self.width // n_date
        self.pix = min(16, self.cols)
        self.halves = self.cols // self.pix
        assert self.halves <= 2
        self.groups = LANES // self.pix
        self.blocks = DATES // self.groups
        self.per = 2 if self.blocks % 2 == 0 else 1
        self.span = self.pix + 2 * RIM
        self.left = [d for d in range(n_date) if d * self.cols < RIM]
        self.right = [n_date - 1 - d for d in self.left]
        if self.halves == 2:
            self.pieces = [(0, self.pix), (LINES * self.pix, 2 * RIM), (PART, self.pix)]
            self.tail, self.stride = PART, PART + LANES
        else:
            self.pieces = [(0, self.span)]
            self.tail, self.stride = 0, PART
        self.tail_width = self.pieces[-1][1]
        self.tail_lanes = self.stride - self.tail

    def chunk(self, date):
        odd = lax.rem(lax.axis_index("space"), 2) == 1
        return jnp.where(odd, self.n_date - 1 - date, date)

    def swapped(self, chunk):
        return chunk <= self.left[-1]

    def half(self, chunk, slot):
        if self.halves == 1:
            return 0
        return jnp.where(self.swapped(chunk), 1 - slot, slot)


def pack_kernel(plan, x_ref, *refs):
    n_date, width = plan.n_date, plan.width
    main, plane = refs[:n_date], refs[n_date]
    me = lax.axis_index("date")
    plane[...] = x_ref[...].astype(f32)
    lane = lax.broadcasted_iota(jnp.int32, (1, LANES), 1)
    tile_count = plan.stride // LANES

    def place(tiles, part, base, wide, first, low, high):
        for line in range(LINES):
            start = base + line * wide
            moved = pltpu.roll(plane[part, line], lax.rem(start - first + 8 * LANES, LANES), 1)
            for tile in range(tile_count):
                if start < (tile + 1) * LANES and start + wide > tile * LANES:
                    at = lane + (tile * LANES - start)
                    tiles[tile] = jnp.where((at >= low) & (at < high), moved, tiles[tile])

    for r in range(n_date):
        chunk = plan.chunk(lax.rem(me + r, n_date))
        swapped = plan.swapped(chunk)
        window = chunk * plan.cols - RIM
        far = window + plan.span
        for part in range(2):
            tiles = [jnp.zeros((plan.own, LANES), f32) for _ in range(tile_count)]
            for k, (base, wide) in enumerate(plan.pieces):
                if len(plan.pieces) == 1:
                    first = window
                elif k == 1:
                    first = window + plan.pix
                else:
                    first = jnp.where(swapped == (k == 2), window, far)
                low, high = jnp.maximum(0, -first), jnp.minimum(wide, width - first)
                place(tiles, part, base, wide, first, low, high)
            base, wide = plan.pieces[-1]
            place(
                tiles,
                part,
                base,
                wide,
                jnp.where(swapped, 0, width - wide),
                jnp.where(swapped, 0, jnp.minimum(wide, width - first)),
                jnp.where(swapped, -first, wide),
            )
            for k, tile in enumerate(tiles):
                at = part * plan.stride + k * LANES
                main[r][:, at : at + LANES] = tile.astype(bf16)


def unpack_kernel(plan, *refs):
    n_date, own = plan.n_date, plan.own
    pieces, out_ref = refs[:n_date], refs[n_date]
    me = lax.axis_index("date")
    region = LANES // 4
    owner = lax.broadcasted_iota(jnp.int32, (1, LANES), 1) // plan.cols
    for quarter in range(4):
        value = jnp.zeros((own // 2, LANES), f32)
        for r in range(n_date):
            chunk = plan.chunk(lax.rem(me + n_date - r, n_date))
            shift = lax.rem(chunk * plan.cols // region + 4 - quarter, 4) * region
            value = jnp.where(owner == chunk, pltpu.roll(pieces[r][...], shift, 1), value)
        start = quarter % 2 * (own // 2)
        out_ref[quarter // 2, start : start + own // 2, :] = value


def group_sum(x, pix):
    step = LANES // 2
    while step >= pix:
        x = x + pltpu.roll(x, step, 1)
        step //= 2
    return x


def link_kernel(plan, slot, *refs):
    n_date, own, pix = plan.n_date, plan.own, plan.pix
    groups, blocks, per, span = plan.groups, plan.blocks, plan.per, plan.span
    last = slot == plan.halves - 1
    main, days_ref, refs = refs[:n_date], refs[n_date], refs[n_date + 1 :]
    edge_ref = before_ref = None
    if last:
        edge_ref, refs = refs[0], refs[1:]
        if slot:
            before_ref, refs = refs[0], refs[1:]
    outs, refs = refs[: n_date if last else 1], refs[n_date if last else 1 :]
    (s_ref, left_ref, high_ref, low_ref, a_ref, raw_ref, cr_ref, ci_ref, ca_ref,
     mr_ref, mi_ref, ms_ref, y_ref, v_ref, ty_ref, tv_ref, a2_ref, raw2_ref) = refs
    me = lax.axis_index("date")
    chunk = plan.chunk(me)
    nt = (((1,), (1,)), ((), ()))
    rows = [slice(b, b + 40) for b in range(0, DATES, 40)]
    sub = lax.broadcasted_iota(jnp.int32, (groups, LANES), 0)
    lane = lax.broadcasted_iota(jnp.int32, (groups, LANES), 1)
    diag = jnp.where(lane // pix == sub, 1.0, 0.0).astype(f32)

    spot = lax.broadcasted_iota(jnp.int32, (16, PART), 1)
    if plan.halves == 1:
        layout = [(0, span, 0)]
    elif last:
        layout = [(0, 2 * RIM, plan.pix), (plan.tail - plan.pieces[1][0], pix, jnp.where(plan.swapped(chunk), 0, span))]
    else:
        layout = [(0, pix, jnp.where(plan.swapped(chunk), span, 0)), (plan.pieces[1][0], 2 * RIM, plan.pix)]
    column = jnp.full((16, PART), -LANES, jnp.int32)
    for base, wide, col in layout:
        for line in range(LINES):
            start = base + line * wide
            column = jnp.where((spot >= start) & (spot < start + wide), spot - start + col, column)
    column = column - plan.half(chunk, slot) * pix
    offset = column - lax.rem(lax.broadcasted_iota(jnp.int32, (16, PART), 0), pix)
    inside = jnp.where((offset >= 0) & (offset <= 2 * RIM), 1.0, 0.0).astype(f32)
    mask = jnp.concatenate([inside, inside], axis=1).astype(bf16)
    rep = jnp.concatenate([inside] * (LANES // 16), axis=0).astype(bf16)

    def to_rows(y):
        return [
            jnp.sum(y[b * groups : (b + 1) * groups] * diag, axis=0, keepdims=True) for b in range(blocks)
        ]

    for r in range(n_date):
        for part in range(2):
            s = main[r][:, part * plan.stride : (part + 1) * plan.stride].astype(f32)
            if slot:
                s = pltpu.roll(s, plan.stride - plan.pieces[1][0], 1)
            s_ref[r * own : (r + 1) * own, part * PART : (part + 1) * PART] = s[:, 0:PART]
    if last:
        is_left = plan.swapped(chunk)
        depth = jnp.where(is_left, chunk, n_date - 1 - chunk)
        missing = RIM - depth * plan.cols
        wide = plan.tail_width
        base = plan.tail - plan.pieces[1][0] if plan.halves == 2 else 0

        @pl.when(missing > 0)
        def _():
            at = lax.broadcasted_iota(jnp.int32, (1, PART), 1) - base
            col = at
            for _line in range(1, LINES):
                col = jnp.where(col >= wide, col - wide, col)
            low = jnp.where(is_left, 0, wide - missing)
            valid = (col >= low) & (col < low + missing) & (at >= 0) & (at < LINES * wide)
            outermost = lax.axis_index("space") == jnp.where(is_left, 0, lax.axis_size("space") - 1)
            shift = jnp.where(is_left, missing - wide, wide - missing) + base
            for part in range(2):
                got = edge_ref[:, part * plan.tail_lanes : (part + 1) * plan.tail_lanes].astype(f32)
                if plan.tail_lanes < PART:
                    got = jnp.concatenate([got, jnp.zeros((DATES, PART - plan.tail_lanes), f32)], axis=1)
                got = jnp.where(outermost, 0.0, pltpu.roll(got, lax.rem(shift + PART, PART), 1))
                at_part = slice(part * PART, (part + 1) * PART)
                s_ref[:, at_part] = jnp.where(valid, got, s_ref[:, at_part])

    sub8 = lax.broadcasted_iota(jnp.int32, (8, LANES), 0)
    for b in range(0, DATES, 8):
        days = jnp.zeros((8, LANES), f32)
        for t in range(8):
            r, at = divmod(b + t, own)
            day = days_ref[lax.rem(me + n_date - r, n_date) * own + at].astype(f32)
            days = jnp.where(sub8 == t, day, days)
        ty_ref[0, b : b + 8] = jnp.exp(days * (1.0 / taper_days))
        ty_ref[1, b : b + 8] = jnp.exp(days * (-1.0 / taper_days))
    sr, si = s_ref[:, 0:PART], s_ref[:, PART : 2 * PART]
    left_ref[0:DATES, 0:PART] = sr.astype(bf16)
    left_ref[0:DATES, PART : 2 * PART] = si.astype(bf16)
    left_ref[DATES : 2 * DATES, 0:PART] = si.astype(bf16)
    left_ref[DATES : 2 * DATES, PART : 2 * PART] = (-sr).astype(bf16)
    left_ref[:, 2 * PART :] = left_ref[:, : 2 * PART]
    intensity = sr * sr + si * si
    weight = 1.0 / (jnp.sum(intensity, axis=0, keepdims=True) / DATES + epsilon)
    for part, s in enumerate((sr, si)):
        at = slice(part * PART, (part + 1) * PART)
        scaled = s * weight
        high = scaled.astype(bf16).astype(f32)
        high_ref[:, at] = high
        low_ref[:, at] = scaled - high
    weighted = intensity * weight
    high = weighted.astype(bf16)
    low = (weighted - high.astype(f32)).astype(bf16)
    power = lax.dot_general(high, rep, nt, preferred_element_type=f32)
    power = power + lax.dot_general(low, rep, nt, preferred_element_type=f32)
    root = lax.rsqrt(power + epsilon)
    for k in range(2):
        y = ty_ref[k] * root
        ty_ref[k] = y
        for b, row in enumerate(to_rows(y)):
            tv_ref[k, b : b + 1, :] = row

    unit = max(1, 16 // pix)

    def build(first, a_ref):
        for p in range(per):
            for g in range(0, groups, unit):
                for k, ref in enumerate((high_ref, low_ref)):
                    rows16 = jnp.concatenate(
                        [
                            jnp.broadcast_to(ref[pl.ds((first + p) * groups + g + u, 1), :], (pix, 2 * PART))
                            for u in range(unit)
                        ],
                        axis=0,
                    )
                    at = p * LANES + g * pix
                    a_ref[at : at + 16, k * 2 * PART : (k + 1) * 2 * PART] = rows16.astype(bf16) * mask

    def multiply(a_ref, raw_ref):
        raw_ref[...] = lax.dot_general(left_ref[...], a_ref[...], nt, preferred_element_type=f32)

    def normalise(first, raw_ref):
        for p in range(per):
            b = first + p
            grow_row = tv_ref[0, pl.ds(b, 1), :]
            decay_row = tv_ref[1, pl.ds(b, 1), :]
            at = slice(p * LANES, (p + 1) * LANES)
            sum_r = jnp.zeros((8, LANES), f32)
            sum_i = jnp.zeros((8, LANES), f32)
            for part in rows:
                shifted = slice(part.start + DATES, part.stop + DATES)
                factor = jnp.minimum(ty_ref[0, part] * decay_row, ty_ref[1, part] * grow_row)
                cr = raw_ref[part, at] * factor
                ci = raw_ref[shifted, at] * factor
                square = cr * cr + ci * ci
                cr_ref[b, part, :] = cr
                ci_ref[b, part, :] = ci
                ca_ref[b, part, :] = square * lax.rsqrt(jnp.maximum(square, 1e-36))
                sum_r = sum_r + jnp.sum(cr.reshape(5, 8, LANES), axis=0)
                sum_i = sum_i + jnp.sum(ci.reshape(5, 8, LANES), axis=0)
            at = pl.ds(pl.multiple_of(b * groups, groups), groups)
            y_ref[0, at] = jnp.sum(sum_r, axis=0, keepdims=True) * diag
            y_ref[1, at] = -jnp.sum(sum_i, axis=0, keepdims=True) * diag


    steps = blocks // per

    def coherence(pair, carry):
        step = 2 * pair
        multiply(a2_ref, raw2_ref)
        build((step + 2) * per, a_ref)
        normalise(step * per, raw_ref)
        multiply(a_ref, raw_ref)
        build(jnp.minimum(step + 3, steps - 1) * per, a2_ref)
        normalise((step + 1) * per, raw2_ref)
        return carry

    build(0, a_ref)
    multiply(a_ref, raw_ref)
    build(per, a2_ref)
    for pair in range((steps - 1) // 2):
        coherence(pair, 0)
    if steps % 2 == 0:
        multiply(a2_ref, raw2_ref)
        normalise((steps - 2) * per, raw_ref)
        normalise((steps - 1) * per, raw2_ref)
    else:
        normalise((steps - 1) * per, raw_ref)

    def unit_vector(scale):
        yr = group_sum(y_ref[0], pix) * scale
        yi = group_sum(y_ref[1], pix) * scale
        mean = jnp.sum(yr * yr + yi * yi, axis=0, keepdims=True) / DATES
        inv = lax.rsqrt(mean + epsilon)
        y_ref[0] = yr * inv
        y_ref[1] = yi * inv

    def first_step():
        yr, yi = y_ref[0], y_ref[1]
        square = yr * yr + yi * yi
        y_ref[2] = square * lax.rsqrt(jnp.maximum(square, 1e-36))
        for k in range(3):
            for b, row in enumerate(to_rows(y_ref[k])):
                v_ref[k, b : b + 1, :] = row

        def body(b, carry):
            la = v_ref[2, pl.ds(b, 1), :] * reweight_gain
            lr4 = v_ref[0, pl.ds(b, 1), :] * reweight_gain
            li4 = v_ref[1, pl.ds(b, 1), :] * reweight_gain
            sum_r = jnp.zeros((8, LANES), f32)
            sum_i = jnp.zeros((8, LANES), f32)
            for part in rows:
                cr, ci = cr_ref[b, part, :], ci_ref[b, part, :]
                yr, yi = y_ref[0, part], y_ref[1, part]
                pr = cr * yr + ci * yi
                pi = cr * yi - ci * yr
                den = (1.0 + ca_ref[b, part, :] * (y_ref[2, part] * la)) - (lr4 * pr + li4 * pi)
                g = 1.0 / den
                mr, mi = cr * g, ci * g
                mr_ref[b, part, :] = mr
                mi_ref[b, part, :] = mi
                ms_ref[b, part, :] = mr + mi
                sum_r = sum_r + jnp.sum((pr * g).reshape(5, 8, LANES), axis=0)
                sum_i = sum_i + jnp.sum((pi * g).reshape(5, 8, LANES), axis=0)
            set_row(b, jnp.sum(sum_r, axis=0, keepdims=True), jnp.sum(sum_i, axis=0, keepdims=True))
            return carry

        lax.fori_loop(0, blocks, body, 0, unroll=4 if blocks % 4 == 0 else 2)

    def set_row(b, vr, vi):
        tv_ref[0, pl.ds(b, 1), :] = vr
        tv_ref[1, pl.ds(b, 1), :] = vi

    def rows_to_lanes():
        vr, vi = tv_ref[0], tv_ref[1]
        v_ref[0] = vr
        v_ref[1] = vi - vr
        v_ref[2] = vr + vi
        for part in rows:
            zero = jnp.zeros((40, LANES), f32)

            def body(b, acc, part=part):
                v0, v1, v2 = (v_ref[k, pl.ds(b, 1), :] for k in range(3))
                return (
                    acc[0] + ms_ref[b, part, :] * v0,
                    acc[1] + mr_ref[b, part, :] * v1,
                    acc[2] + mi_ref[b, part, :] * v2,
                )

            k1, k2, k3 = lax.fori_loop(0, blocks, body, (zero, zero, zero), unroll=10)
            y_ref[0, part] = k1 - k3
            y_ref[1, part] = k1 + k2

    def lanes_to_rows():
        yr = group_sum(y_ref[0], pix)
        yi = group_sum(y_ref[1], pix)
        y_ref[0] = yr
        y_ref[1] = yi - yr
        y_ref[2] = yr + yi

        def body(step, carry):
            sums = [[jnp.zeros((8, LANES), f32) for _ in range(3)] for _ in range(per)]
            for part in rows:
                y0, y1, y2 = (y_ref[k, part] for k in range(3))
                for p in range(per):
                    b = step * per + p
                    for k, (m, y) in enumerate(((ms_ref, y0), (mi_ref, y1), (mr_ref, y2))):
                        sums[p][k] += jnp.sum((m[b, part, :] * y).reshape(5, 8, LANES), axis=0)
            for p in range(per):
                k1, k2, k3 = (jnp.sum(s, axis=0, keepdims=True) for s in sums[p])
                set_row(step * per + p, k1 + k2, k3 - k1)
            return carry

        lax.fori_loop(0, blocks // per, body, 0, unroll=2 if blocks // per % 2 == 0 else 1)

    unit_vector(1.0)
    for outer in range(ITERS):
        first_step()
        for step in range(1, POWER):
            if step % 2:
                rows_to_lanes()
            else:
                lanes_to_rows()
        unit_vector(1.0 / math.sqrt(DATES) ** POWER)

    if not last:
        outs[0][...] = y_ref[0:2]
        return
    lane_row = lax.broadcasted_iota(jnp.int32, (1, LANES), 1)
    here = lax.rem(lane_row // pix, plan.halves) == plan.half(chunk, slot)
    quarter = lane_row // (LANES // 4)
    for r in range(n_date):
        value = None
        for q in range(4):
            start = (n_date - r) % n_date * own + q % 2 * (own // 2)
            at = slice(start, start + own // 2)
            piece = y_ref[q // 2, at]
            if slot:
                piece = jnp.where(here, piece, before_ref[q // 2, at])
            value = piece if value is None else jnp.where(quarter == q, piece, value)
        outs[r][...] = value


def link(plan, slot, main, days, *more):
    last = slot == plan.halves - 1
    matrix = pltpu.VMEM((plan.blocks, DATES, LANES), f32)
    samples = pltpu.VMEM((DATES, 2 * PART), f32)
    if last:
        shapes = [jax.ShapeDtypeStruct((plan.own // 2, LANES), f32)] * plan.n_date
    else:
        shapes = [jax.ShapeDtypeStruct((2, DATES, LANES), f32)]
    return pl.pallas_call(
        functools.partial(link_kernel, plan, slot),
        out_shape=shapes,
        in_specs=[VMEM] * plan.n_date + [pl.BlockSpec(memory_space=pltpu.SMEM)] + [VMEM] * len(more),
        out_specs=[VMEM] * len(shapes),
        scratch_shapes=[
            samples,
            pltpu.VMEM((2 * DATES, 4 * PART), bf16),
            samples,
            samples,
            pltpu.VMEM((plan.per * LANES, 4 * PART), bf16),
            pltpu.VMEM((2 * DATES, PART), f32),
        ]
        + [matrix] * 6
        + [
            pltpu.VMEM((3, DATES, LANES), f32),
            pltpu.VMEM((3, plan.blocks, LANES), f32),
            pltpu.VMEM((2, DATES, LANES), f32),
            pltpu.VMEM((2, plan.blocks, LANES), f32),
            pltpu.VMEM((plan.per * LANES, 4 * PART), bf16),
            pltpu.VMEM((2 * DATES, PART), f32),
        ],
        compiler_params=pltpu.CompilerParams(vmem_limit_bytes=24 * 2**20),
    )(*main, days, *more)


def local(acquisitions, acquisition_day):
    n_date, n_space = lax.axis_size("date"), lax.axis_size("space")
    plan = Plan(acquisitions.shape, n_date)
    own = plan.own

    main = pl.pallas_call(
        functools.partial(pack_kernel, plan),
        out_shape=[jax.ShapeDtypeStruct((own, 2 * plan.stride), bf16)] * n_date,
        in_specs=[VMEM],
        out_specs=[VMEM] * n_date,
        scratch_shapes=[pltpu.VMEM((2, LINES, own, LANES), f32)],
        compiler_params=pltpu.CompilerParams(vmem_limit_bytes=24 * 2**20),
    )(jnp.transpose(acquisitions, (0, 2, 1, 3)))
    main = list(main)
    for r in range(1, n_date):
        main[r] = lax.ppermute(main[r], "date", [(i, (i + r) % n_date) for i in range(n_date)])
    swap = []
    for s in range(n_space - 1):
        for d in plan.right if s % 2 == 0 else plan.left:
            before, after = s * n_date + d, (s + 1) * n_date + d
            swap += [(before, after), (after, before)]
    idle = [d for d in range(n_date) if d not in plan.left + plan.right]
    for d in plan.left:
        swap += [(d, (n_space - 1) * n_date + d), ((n_space - 1) * n_date + d, d)]
    for s in range(n_space):
        for one, two in zip(idle[0::2], idle[1::2]):
            swap += [(s * n_date + one, s * n_date + two), (s * n_date + two, s * n_date + one)]
    edge = jnp.concatenate(
        [
            jnp.concatenate([m[:, k * plan.stride + plan.tail : (k + 1) * plan.stride] for k in range(2)], axis=1)
            for m in main
        ],
        axis=0,
    )
    edge = lax.ppermute(edge, ("space", "date"), swap)

    if plan.halves == 1:
        out = link(plan, 0, main, acquisition_day, edge)
    else:
        (before,) = link(plan, 0, main, acquisition_day)
        out = link(plan, 1, main, acquisition_day, edge, before)

    pieces = list(out)
    for k in range(1, n_date):
        pieces[k] = lax.ppermute(out[k], "date", [(i, (i + k) % n_date) for i in range(n_date)])
    return pl.pallas_call(
        functools.partial(unpack_kernel, plan),
        out_shape=jax.ShapeDtypeStruct((2, own, plan.width), f32),
        in_specs=[VMEM] * n_date,
        out_specs=VMEM,
        compiler_params=pltpu.CompilerParams(vmem_limit_bytes=24 * 2**20),
    )(*pieces)


def solution(mesh):
    return jax.shard_map(
        local,
        mesh=mesh,
        in_specs=(P(None, "date", None, "space"), P()),
        out_specs=P(None, "date", "space"),
        check_vma=False,
    )
```

```python
import functools
import math

import jax
import jax.numpy as jnp
from jax import lax
from jax.experimental import pallas as pl
from jax.experimental.pallas import tpu as pltpu
from jax.sharding import PartitionSpec as P

DATES = 160
RIM = 10
LINES = 7
ITERS = 2
POWER = 4
LANES = 128
PART = 256

epsilon = 1e-06
reweight_gain = 4.0
taper_days = 360.0

f32 = jnp.float32
bf16 = jnp.bfloat16
VMEM = pl.BlockSpec(memory_space=pltpu.VMEM)


class Plan:
    def __init__(self, shape, n_date):
        self.n_date = n_date
        self.own = shape[1]
        self.width = shape[3]
        self.cols = self.width // n_date
        self.pix = min(16, self.cols)
        self.halves = self.cols // self.pix
        assert self.halves <= 2
        self.groups = LANES // self.pix
        self.blocks = DATES // self.groups
        self.per = 2 if self.blocks % 2 == 0 else 1
        self.span = self.pix + 2 * RIM
        self.left = [d for d in range(n_date) if d * self.cols < RIM]
        self.right = [n_date - 1 - d for d in self.left]
        if self.halves == 2:
            self.pieces = [(0, self.pix), (LINES * self.pix, 2 * RIM), (PART, self.pix)]
            self.tail, self.stride = PART, PART + LANES
        else:
            self.pieces = [(0, self.span)]
            self.tail, self.stride = 0, PART
        self.tail_width = self.pieces[-1][1]
        self.tail_lanes = self.stride - self.tail

    def chunk(self, date):
        odd = lax.rem(lax.axis_index("space"), 2) == 1
        return jnp.where(odd, self.n_date - 1 - date, date)

    def swapped(self, chunk):
        return chunk <= self.left[-1]

    def half(self, chunk, slot):
        if self.halves == 1:
            return 0
        return jnp.where(self.swapped(chunk), 1 - slot, slot)


def taper_kernel(plan, days_ref, taper):
    n_date = plan.n_date
    me = lax.axis_index("date")
    row = days_ref[...].astype(f32).reshape(1, DATES)
    lane_of = lax.broadcasted_iota(jnp.int32, (8, DATES), 1)
    sub_of = lax.broadcasted_iota(jnp.int32, (8, DATES), 0)
    for r in range(n_date):
        first = lax.rem(me + n_date - r, n_date) * plan.own
        for b in range(0, plan.own, 8):
            high = min(8, plan.own - b)
            picked = jnp.where(lane_of == sub_of + (first + b), row, 0.0)
            days = jnp.sum(picked, axis=1, keepdims=True)[:high]
            at = r * plan.own + b
            taper[0, at : at + high] = jnp.broadcast_to(jnp.exp(days * (1.0 / taper_days)), (high, LANES))
            taper[1, at : at + high] = jnp.broadcast_to(jnp.exp(days * (-1.0 / taper_days)), (high, LANES))


def pack_kernel(plan, x_ref, *refs):
    n_date, width = plan.n_date, plan.width
    main, plane = refs[:n_date], refs[n_date]
    me = lax.axis_index("date")
    plane[...] = x_ref[...].astype(f32)
    lane = lax.broadcasted_iota(jnp.int32, (1, LANES), 1)
    tile_count = plan.stride // LANES

    def place(tiles, part, base, wide, first, low, high):
        for line in range(LINES):
            start = base + line * wide
            moved = pltpu.roll(plane[part, line], lax.rem(start - first + 8 * LANES, LANES), 1)
            for tile in range(tile_count):
                if start < (tile + 1) * LANES and start + wide > tile * LANES:
                    at = lane + (tile * LANES - start)
                    tiles[tile] = jnp.where((at >= low) & (at < high), moved, tiles[tile])

    for r in range(n_date):
        chunk = plan.chunk(lax.rem(me + r, n_date))
        swapped = plan.swapped(chunk)
        window = chunk * plan.cols - RIM
        far = window + plan.span
        for part in range(2):
            tiles = [jnp.zeros((plan.own, LANES), f32) for _ in range(tile_count)]
            for k, (base, wide) in enumerate(plan.pieces):
                if len(plan.pieces) == 1:
                    first = window
                elif k == 1:
                    first = window + plan.pix
                else:
                    first = jnp.where(swapped == (k == 2), window, far)
                low, high = jnp.maximum(0, -first), jnp.minimum(wide, width - first)
                place(tiles, part, base, wide, first, low, high)
            base, wide = plan.pieces[-1]
            place(
                tiles,
                part,
                base,
                wide,
                jnp.where(swapped, 0, width - wide),
                jnp.where(swapped, 0, jnp.minimum(wide, width - first)),
                jnp.where(swapped, -first, wide),
            )
            for k, tile in enumerate(tiles):
                at = part * plan.stride + k * LANES
                main[r][:, at : at + LANES] = tile.astype(bf16)


def unpack_kernel(plan, *refs):
    n_date, own = plan.n_date, plan.own
    pieces, out_ref = refs[:n_date], refs[n_date]
    me = lax.axis_index("date")
    region = LANES // 4
    owner = lax.broadcasted_iota(jnp.int32, (1, LANES), 1) // plan.cols
    for quarter in range(4):
        value = jnp.zeros((own // 2, LANES), f32)
        for r in range(n_date):
            chunk = plan.chunk(lax.rem(me + n_date - r, n_date))
            shift = lax.rem(chunk * plan.cols // region + 4 - quarter, 4) * region
            value = jnp.where(owner == chunk, pltpu.roll(pieces[r][...], shift, 1), value)
        start = quarter % 2 * (own // 2)
        out_ref[quarter // 2, start : start + own // 2, :] = value


def group_sum(x, pix):
    step = LANES // 2
    while step >= pix:
        x = x + pltpu.roll(x, step, 1)
        step //= 2
    return x


def link_kernel(plan, slot, *refs):
    n_date, own, pix = plan.n_date, plan.own, plan.pix
    groups, blocks, per, span = plan.groups, plan.blocks, plan.per, plan.span
    last = slot == plan.halves - 1
    main, taper_ref, refs = refs[:n_date], refs[n_date], refs[n_date + 1 :]
    edge_ref = before_ref = None
    if last:
        edge_ref, refs = refs[0], refs[1:]
        if slot:
            before_ref, refs = refs[0], refs[1:]
    outs, refs = refs[: n_date if last else 1], refs[n_date if last else 1 :]
    (s_ref, left_ref, high_ref, low_ref, a_ref, raw_ref, cr_ref, ci_ref, ca_ref,
     mr_ref, mi_ref, ms_ref, y_ref, v_ref, ty_ref, tv_ref, a2_ref, raw2_ref) = refs
    me = lax.axis_index("date")
    chunk = plan.chunk(me)
    nt = (((1,), (1,)), ((), ()))
    rows = [slice(b, b + 40) for b in range(0, DATES, 40)]
    sub = lax.broadcasted_iota(jnp.int32, (groups, LANES), 0)
    lane = lax.broadcasted_iota(jnp.int32, (groups, LANES), 1)
    diag = jnp.where(lane // pix == sub, 1.0, 0.0).astype(f32)

    spot = lax.broadcasted_iota(jnp.int32, (16, PART), 1)
    if plan.halves == 1:
        layout = [(0, span, 0)]
    elif last:
        layout = [(0, 2 * RIM, plan.pix), (plan.tail - plan.pieces[1][0], pix, jnp.where(plan.swapped(chunk), 0, span))]
    else:
        layout = [(0, pix, jnp.where(plan.swapped(chunk), span, 0)), (plan.pieces[1][0], 2 * RIM, plan.pix)]
    column = jnp.full((16, PART), -LANES, jnp.int32)
    for base, wide, col in layout:
        for line in range(LINES):
            start = base + line * wide
            column = jnp.where((spot >= start) & (spot < start + wide), spot - start + col, column)
    column = column - plan.half(chunk, slot) * pix
    offset = column - lax.rem(lax.broadcasted_iota(jnp.int32, (16, PART), 0), pix)
    inside = jnp.where((offset >= 0) & (offset <= 2 * RIM), 1.0, 0.0).astype(f32)
    mask = jnp.concatenate([inside, inside], axis=1).astype(bf16)
    rep = jnp.concatenate([inside] * (LANES // 16), axis=0).astype(bf16)

    def to_rows(y):
        return [
            jnp.sum(y[b * groups : (b + 1) * groups] * diag, axis=0, keepdims=True) for b in range(blocks)
        ]

    for r in range(n_date):
        for part in range(2):
            s = main[r][:, part * plan.stride : (part + 1) * plan.stride].astype(f32)
            if slot:
                s = pltpu.roll(s, plan.stride - plan.pieces[1][0], 1)
            s_ref[r * own : (r + 1) * own, part * PART : (part + 1) * PART] = s[:, 0:PART]
    if last:
        is_left = plan.swapped(chunk)
        depth = jnp.where(is_left, chunk, n_date - 1 - chunk)
        missing = RIM - depth * plan.cols
        wide = plan.tail_width
        base = plan.tail - plan.pieces[1][0] if plan.halves == 2 else 0

        @pl.when(missing > 0)
        def _():
            at = lax.broadcasted_iota(jnp.int32, (1, PART), 1) - base
            col = at
            for _line in range(1, LINES):
                col = jnp.where(col >= wide, col - wide, col)
            low = jnp.where(is_left, 0, wide - missing)
            valid = (col >= low) & (col < low + missing) & (at >= 0) & (at < LINES * wide)
            outermost = lax.axis_index("space") == jnp.where(is_left, 0, lax.axis_size("space") - 1)
            shift = jnp.where(is_left, missing - wide, wide - missing) + base
            for part in range(2):
                got = edge_ref[:, part * plan.tail_lanes : (part + 1) * plan.tail_lanes].astype(f32)
                if plan.tail_lanes < PART:
                    got = jnp.concatenate([got, jnp.zeros((DATES, PART - plan.tail_lanes), f32)], axis=1)
                got = jnp.where(outermost, 0.0, pltpu.roll(got, lax.rem(shift + PART, PART), 1))
                at_part = slice(part * PART, (part + 1) * PART)
                s_ref[:, at_part] = jnp.where(valid, got, s_ref[:, at_part])

    sr, si = s_ref[:, 0:PART], s_ref[:, PART : 2 * PART]
    left_ref[0:DATES, 0:PART] = sr.astype(bf16)
    left_ref[0:DATES, PART : 2 * PART] = si.astype(bf16)
    left_ref[DATES : 2 * DATES, 0:PART] = si.astype(bf16)
    left_ref[DATES : 2 * DATES, PART : 2 * PART] = (-sr).astype(bf16)
    left_ref[:, 2 * PART :] = left_ref[:, : 2 * PART]
    intensity = sr * sr + si * si
    weight = 1.0 / (jnp.sum(intensity, axis=0, keepdims=True) / DATES + epsilon)
    for part, s in enumerate((sr, si)):
        at = slice(part * PART, (part + 1) * PART)
        scaled = s * weight
        high = scaled.astype(bf16).astype(f32)
        high_ref[:, at] = high
        low_ref[:, at] = scaled - high
    weighted = intensity * weight
    high = weighted.astype(bf16)
    low = (weighted - high.astype(f32)).astype(bf16)
    power = lax.dot_general(high, rep, nt, preferred_element_type=f32)
    power = power + lax.dot_general(low, rep, nt, preferred_element_type=f32)
    root = lax.rsqrt(power + epsilon)
    for k in range(2):
        y = taper_ref[k] * root
        ty_ref[k] = y
        for b, row in enumerate(to_rows(y)):
            tv_ref[k, b : b + 1, :] = row

    unit = max(1, 16 // pix)

    def build(first, a_ref):
        for p in range(per):
            for g in range(0, groups, unit):
                for k, ref in enumerate((high_ref, low_ref)):
                    rows16 = jnp.concatenate(
                        [
                            jnp.broadcast_to(ref[pl.ds((first + p) * groups + g + u, 1), :], (pix, 2 * PART))
                            for u in range(unit)
                        ],
                        axis=0,
                    )
                    at = p * LANES + g * pix
                    a_ref[at : at + 16, k * 2 * PART : (k + 1) * 2 * PART] = rows16.astype(bf16) * mask

    def multiply(a_ref, raw_ref):
        raw_ref[...] = lax.dot_general(left_ref[...], a_ref[...], nt, preferred_element_type=f32)

    def normalise(first, raw_ref):
        for p in range(per):
            b = first + p
            grow_row = tv_ref[0, pl.ds(b, 1), :]
            decay_row = tv_ref[1, pl.ds(b, 1), :]
            at = slice(p * LANES, (p + 1) * LANES)
            sum_r = jnp.zeros((8, LANES), f32)
            sum_i = jnp.zeros((8, LANES), f32)
            for part in rows:
                shifted = slice(part.start + DATES, part.stop + DATES)
                factor = jnp.minimum(ty_ref[0, part] * decay_row, ty_ref[1, part] * grow_row)
                cr = raw_ref[part, at] * factor
                ci = raw_ref[shifted, at] * factor
                square = cr * cr + ci * ci
                cr_ref[b, part, :] = cr
                ci_ref[b, part, :] = ci
                ca_ref[b, part, :] = square * lax.rsqrt(jnp.maximum(square, 1e-36))
                sum_r = sum_r + jnp.sum(cr.reshape(5, 8, LANES), axis=0)
                sum_i = sum_i + jnp.sum(ci.reshape(5, 8, LANES), axis=0)
            at = pl.ds(pl.multiple_of(b * groups, groups), groups)
            y_ref[0, at] = jnp.sum(sum_r, axis=0, keepdims=True) * diag
            y_ref[1, at] = -jnp.sum(sum_i, axis=0, keepdims=True) * diag


    steps = blocks // per

    def coherence(pair, carry):
        step = 2 * pair
        multiply(a2_ref, raw2_ref)
        build((step + 2) * per, a_ref)
        normalise(step * per, raw_ref)
        multiply(a_ref, raw_ref)
        build(jnp.minimum(step + 3, steps - 1) * per, a2_ref)
        normalise((step + 1) * per, raw2_ref)
        return carry

    build(0, a_ref)
    multiply(a_ref, raw_ref)
    build(per, a2_ref)
    for pair in range((steps - 1) // 2):
        coherence(pair, 0)
    if steps % 2 == 0:
        multiply(a2_ref, raw2_ref)
        normalise((steps - 2) * per, raw_ref)
        normalise((steps - 1) * per, raw2_ref)
    else:
        normalise((steps - 1) * per, raw_ref)

    def unit_vector(scale):
        yr = group_sum(y_ref[0], pix) * scale
        yi = group_sum(y_ref[1], pix) * scale
        mean = jnp.sum(yr * yr + yi * yi, axis=0, keepdims=True) / DATES
        inv = lax.rsqrt(mean + epsilon)
        y_ref[0] = yr * inv
        y_ref[1] = yi * inv

    def first_step():
        yr, yi = y_ref[0], y_ref[1]
        square = yr * yr + yi * yi
        y_ref[2] = square * lax.rsqrt(jnp.maximum(square, 1e-36))
        for k in range(3):
            for b, row in enumerate(to_rows(y_ref[k])):
                v_ref[k, b : b + 1, :] = row

        def body(b, carry):
            la = v_ref[2, pl.ds(b, 1), :] * reweight_gain
            lr4 = v_ref[0, pl.ds(b, 1), :] * reweight_gain
            li4 = v_ref[1, pl.ds(b, 1), :] * reweight_gain
            sum_r = jnp.zeros((8, LANES), f32)
            sum_i = jnp.zeros((8, LANES), f32)
            for part in rows:
                cr, ci = cr_ref[b, part, :], ci_ref[b, part, :]
                yr, yi = y_ref[0, part], y_ref[1, part]
                pr = cr * yr + ci * yi
                pi = cr * yi - ci * yr
                den = (1.0 + ca_ref[b, part, :] * (y_ref[2, part] * la)) - (lr4 * pr + li4 * pi)
                g = 1.0 / den
                mr, mi = cr * g, ci * g
                mr_ref[b, part, :] = mr
                mi_ref[b, part, :] = mi
                ms_ref[b, part, :] = mr + mi
                sum_r = sum_r + jnp.sum((pr * g).reshape(5, 8, LANES), axis=0)
                sum_i = sum_i + jnp.sum((pi * g).reshape(5, 8, LANES), axis=0)
            set_row(b, jnp.sum(sum_r, axis=0, keepdims=True), jnp.sum(sum_i, axis=0, keepdims=True))
            return carry

        lax.fori_loop(0, blocks, body, 0, unroll=4 if blocks % 4 == 0 else 2)

    def set_row(b, vr, vi):
        tv_ref[0, pl.ds(b, 1), :] = vr
        tv_ref[1, pl.ds(b, 1), :] = vi

    def rows_to_lanes():
        vr, vi = tv_ref[0], tv_ref[1]
        v_ref[0] = vr
        v_ref[1] = vi - vr
        v_ref[2] = vr + vi
        for part in rows:
            zero = jnp.zeros((40, LANES), f32)

            def body(b, acc, part=part):
                v0, v1, v2 = (v_ref[k, pl.ds(b, 1), :] for k in range(3))
                return (
                    acc[0] + ms_ref[b, part, :] * v0,
                    acc[1] + mr_ref[b, part, :] * v1,
                    acc[2] + mi_ref[b, part, :] * v2,
                )

            k1, k2, k3 = lax.fori_loop(0, blocks, body, (zero, zero, zero), unroll=10)
            y_ref[0, part] = k1 - k3
            y_ref[1, part] = k1 + k2

    def lanes_to_rows():
        yr = group_sum(y_ref[0], pix)
        yi = group_sum(y_ref[1], pix)
        y_ref[0] = yr
        y_ref[1] = yi - yr
        y_ref[2] = yr + yi

        def body(step, carry):
            sums = [[jnp.zeros((8, LANES), f32) for _ in range(3)] for _ in range(per)]
            for part in rows:
                y0, y1, y2 = (y_ref[k, part] for k in range(3))
                for p in range(per):
                    b = step * per + p
                    for k, (m, y) in enumerate(((ms_ref, y0), (mi_ref, y1), (mr_ref, y2))):
                        sums[p][k] += jnp.sum((m[b, part, :] * y).reshape(5, 8, LANES), axis=0)
            for p in range(per):
                k1, k2, k3 = (jnp.sum(s, axis=0, keepdims=True) for s in sums[p])
                set_row(step * per + p, k1 + k2, k3 - k1)
            return carry

        lax.fori_loop(0, blocks // per, body, 0, unroll=2 if blocks // per % 2 == 0 else 1)

    unit_vector(1.0)
    for outer in range(ITERS):
        first_step()
        for step in range(1, POWER):
            if step % 2:
                rows_to_lanes()
            else:
                lanes_to_rows()
        unit_vector(1.0 / math.sqrt(DATES) ** POWER)

    if not last:
        outs[0][...] = y_ref[0:2]
        return
    lane_row = lax.broadcasted_iota(jnp.int32, (1, LANES), 1)
    here = lax.rem(lane_row // pix, plan.halves) == plan.half(chunk, slot)
    quarter = lane_row // (LANES // 4)
    for r in range(n_date):
        value = None
        for q in range(4):
            start = (n_date - r) % n_date * own + q % 2 * (own // 2)
            at = slice(start, start + own // 2)
            piece = y_ref[q // 2, at]
            if slot:
                piece = jnp.where(here, piece, before_ref[q // 2, at])
            value = piece if value is None else jnp.where(quarter == q, piece, value)
        outs[r][...] = value


def link(plan, slot, main, taper, *more):
    last = slot == plan.halves - 1
    matrix = pltpu.VMEM((plan.blocks, DATES, LANES), f32)
    samples = pltpu.VMEM((DATES, 2 * PART), f32)
    if last:
        shapes = [jax.ShapeDtypeStruct((plan.own // 2, LANES), f32)] * plan.n_date
    else:
        shapes = [jax.ShapeDtypeStruct((2, DATES, LANES), f32)]
    return pl.pallas_call(
        functools.partial(link_kernel, plan, slot),
        out_shape=shapes,
        in_specs=[VMEM] * (plan.n_date + 1 + len(more)),
        out_specs=[VMEM] * len(shapes),
        scratch_shapes=[
            samples,
            pltpu.VMEM((2 * DATES, 4 * PART), bf16),
            samples,
            samples,
            pltpu.VMEM((plan.per * LANES, 4 * PART), bf16),
            pltpu.VMEM((2 * DATES, PART), f32),
        ]
        + [matrix] * 6
        + [
            pltpu.VMEM((3, DATES, LANES), f32),
            pltpu.VMEM((3, plan.blocks, LANES), f32),
            pltpu.VMEM((2, DATES, LANES), f32),
            pltpu.VMEM((2, plan.blocks, LANES), f32),
            pltpu.VMEM((plan.per * LANES, 4 * PART), bf16),
            pltpu.VMEM((2 * DATES, PART), f32),
        ],
        compiler_params=pltpu.CompilerParams(vmem_limit_bytes=24 * 2**20),
    )(*main, taper, *more)


def local(acquisitions, acquisition_day):
    n_date, n_space = lax.axis_size("date"), lax.axis_size("space")
    plan = Plan(acquisitions.shape, n_date)
    own = plan.own

    main = pl.pallas_call(
        functools.partial(pack_kernel, plan),
        out_shape=[jax.ShapeDtypeStruct((own, 2 * plan.stride), bf16)] * n_date,
        in_specs=[VMEM],
        out_specs=[VMEM] * n_date,
        scratch_shapes=[pltpu.VMEM((2, LINES, own, LANES), f32)],
        compiler_params=pltpu.CompilerParams(vmem_limit_bytes=24 * 2**20),
    )(jnp.transpose(acquisitions, (0, 2, 1, 3)))
    main = list(main)
    main[0], acquisition_day = lax.optimization_barrier((main[0], acquisition_day))
    taper = pl.pallas_call(
        functools.partial(taper_kernel, plan),
        out_shape=jax.ShapeDtypeStruct((2, DATES, LANES), f32),
        in_specs=[VMEM],
        out_specs=VMEM,
    )(acquisition_day)
    main[0], taper = lax.optimization_barrier((main[0], taper))
    for r in range(1, n_date):
        main[r] = lax.ppermute(main[r], "date", [(i, (i + r) % n_date) for i in range(n_date)])
    swap = []
    for s in range(n_space - 1):
        for d in plan.right if s % 2 == 0 else plan.left:
            before, after = s * n_date + d, (s + 1) * n_date + d
            swap += [(before, after), (after, before)]
    idle = [d for d in range(n_date) if d not in plan.left + plan.right]
    for d in plan.left:
        swap += [(d, (n_space - 1) * n_date + d), ((n_space - 1) * n_date + d, d)]
    for s in range(n_space):
        for one, two in zip(idle[0::2], idle[1::2]):
            swap += [(s * n_date + one, s * n_date + two), (s * n_date + two, s * n_date + one)]
    edge = jnp.concatenate(
        [
            jnp.concatenate([m[:, k * plan.stride + plan.tail : (k + 1) * plan.stride] for k in range(2)], axis=1)
            for m in main
        ],
        axis=0,
    )
    edge = lax.ppermute(edge, ("space", "date"), swap)

    if plan.halves == 1:
        out = link(plan, 0, main, taper, edge)
    else:
        (before,) = link(plan, 0, main, taper)
        out = link(plan, 1, main, taper, edge, before)

    pieces = list(out)
    for k in range(1, n_date):
        pieces[k] = lax.ppermute(out[k], "date", [(i, (i + k) % n_date) for i in range(n_date)])
    return pl.pallas_call(
        functools.partial(unpack_kernel, plan),
        out_shape=jax.ShapeDtypeStruct((2, own, plan.width), f32),
        in_specs=[VMEM] * n_date,
        out_specs=VMEM,
        compiler_params=pltpu.CompilerParams(vmem_limit_bytes=24 * 2**20),
    )(*pieces)


def solution(mesh):
    return jax.shard_map(
        local,
        mesh=mesh,
        in_specs=(P(None, "date", None, "space"), P()),
        out_specs=P(None, "date", "space"),
        check_vma=False,
    )
```

```python
import functools
import math

import jax
import jax.numpy as jnp
from jax import lax
from jax.experimental import pallas as pl
from jax.experimental.pallas import tpu as pltpu
from jax.sharding import PartitionSpec as P

DATES = 160
RIM = 10
LINES = 7
ITERS = 2
POWER = 4
LANES = 128
PART = 256

epsilon = 1e-06
reweight_gain = 4.0
taper_days = 360.0

f32 = jnp.float32
bf16 = jnp.bfloat16
VMEM = pl.BlockSpec(memory_space=pltpu.VMEM)


class Plan:
    def __init__(self, shape, n_date):
        self.n_date = n_date
        self.own = shape[1]
        self.width = shape[3]
        self.cols = self.width // n_date
        self.pix = min(16, self.cols)
        self.halves = self.cols // self.pix
        assert self.halves <= 2
        self.groups = LANES // self.pix
        self.blocks = DATES // self.groups
        self.per = 2 if self.blocks % 2 == 0 else 1
        self.span = self.pix + 2 * RIM
        self.left = [d for d in range(n_date) if d * self.cols < RIM]
        self.right = [n_date - 1 - d for d in self.left]
        if self.halves == 2:
            self.pieces = [(0, self.pix), (LINES * self.pix, 2 * RIM), (PART, self.pix)]
            self.tail, self.stride = PART, PART + LANES
        else:
            self.pieces = [(0, self.span)]
            self.tail, self.stride = 0, PART
        self.tail_width = self.pieces[-1][1]
        self.tail_lanes = self.stride - self.tail

    def chunk(self, date):
        odd = lax.rem(lax.axis_index("space"), 2) == 1
        return jnp.where(odd, self.n_date - 1 - date, date)

    def swapped(self, chunk):
        return chunk <= self.left[-1]

    def half(self, chunk, slot):
        if self.halves == 1:
            return 0
        return jnp.where(self.swapped(chunk), 1 - slot, slot)


def pack_kernel(plan, steps, x_ref, *refs):
    n_date, width = plan.n_date, plan.width
    main, plane = refs[:-1], refs[-1]
    me = lax.axis_index("date")
    plane[...] = x_ref[...].astype(f32)
    lane = lax.broadcasted_iota(jnp.int32, (1, LANES), 1)
    tile_count = plan.stride // LANES

    def place(tiles, part, base, wide, first, low, high):
        for line in range(LINES):
            start = base + line * wide
            moved = pltpu.roll(plane[part, line], lax.rem(start - first + 8 * LANES, LANES), 1)
            for tile in range(tile_count):
                if start < (tile + 1) * LANES and start + wide > tile * LANES:
                    at = lane + (tile * LANES - start)
                    tiles[tile] = jnp.where((at >= low) & (at < high), moved, tiles[tile])

    for slot, r in enumerate(steps):
        chunk = plan.chunk(lax.rem(me + r, n_date))
        swapped = plan.swapped(chunk)
        window = chunk * plan.cols - RIM
        far = window + plan.span
        for part in range(2):
            tiles = [jnp.zeros((plan.own, LANES), f32) for _ in range(tile_count)]
            for k, (base, wide) in enumerate(plan.pieces):
                if len(plan.pieces) == 1:
                    first = window
                elif k == 1:
                    first = window + plan.pix
                else:
                    first = jnp.where(swapped == (k == 2), window, far)
                low, high = jnp.maximum(0, -first), jnp.minimum(wide, width - first)
                place(tiles, part, base, wide, first, low, high)
            base, wide = plan.pieces[-1]
            place(
                tiles,
                part,
                base,
                wide,
                jnp.where(swapped, 0, width - wide),
                jnp.where(swapped, 0, jnp.minimum(wide, width - first)),
                jnp.where(swapped, -first, wide),
            )
            for k, tile in enumerate(tiles):
                at = part * plan.stride + k * LANES
                main[slot][:, at : at + LANES] = tile.astype(bf16)


def own_kernel(plan, x_ref, days_ref, main, taper, plane):
    pack_kernel(plan, [0], x_ref, main, plane)
    n_date = plan.n_date
    me = lax.axis_index("date")
    row = days_ref[...].astype(f32).reshape(1, DATES)
    lane_of = lax.broadcasted_iota(jnp.int32, (8, DATES), 1)
    sub_of = lax.broadcasted_iota(jnp.int32, (8, DATES), 0)
    for r in range(n_date):
        first = lax.rem(me + n_date - r, n_date) * plan.own
        for b in range(0, plan.own, 8):
            high = min(8, plan.own - b)
            picked = jnp.where(lane_of == sub_of + (first + b), row, 0.0)
            days = jnp.sum(picked, axis=1, keepdims=True)[:high]
            at = r * plan.own + b
            taper[0, at : at + high] = jnp.broadcast_to(jnp.exp(days * (1.0 / taper_days)), (high, LANES))
            taper[1, at : at + high] = jnp.broadcast_to(jnp.exp(days * (-1.0 / taper_days)), (high, LANES))


def unpack_kernel(plan, *refs):
    n_date, own = plan.n_date, plan.own
    pieces, out_ref = refs[:n_date], refs[n_date]
    me = lax.axis_index("date")
    region = LANES // 4
    owner = lax.broadcasted_iota(jnp.int32, (1, LANES), 1) // plan.cols
    for quarter in range(4):
        value = jnp.zeros((own // 2, LANES), f32)
        for r in range(n_date):
            chunk = plan.chunk(lax.rem(me + n_date - r, n_date))
            shift = lax.rem(chunk * plan.cols // region + 4 - quarter, 4) * region
            value = jnp.where(owner == chunk, pltpu.roll(pieces[r][...], shift, 1), value)
        start = quarter % 2 * (own // 2)
        out_ref[quarter // 2, start : start + own // 2, :] = value


def group_sum(x, pix):
    step = LANES // 2
    while step >= pix:
        x = x + pltpu.roll(x, step, 1)
        step //= 2
    return x


def link_kernel(plan, slot, *refs):
    n_date, own, pix = plan.n_date, plan.own, plan.pix
    groups, blocks, per, span = plan.groups, plan.blocks, plan.per, plan.span
    last = slot == plan.halves - 1
    main, taper_ref, refs = refs[:n_date], refs[n_date], refs[n_date + 1 :]
    edge_ref = before_ref = None
    if last:
        edge_ref, refs = refs[0], refs[1:]
        if slot:
            before_ref, refs = refs[0], refs[1:]
    outs, refs = refs[: n_date if last else 1], refs[n_date if last else 1 :]
    (s_ref, left_ref, high_ref, low_ref, a_ref, raw_ref, cr_ref, ci_ref, ca_ref,
     mr_ref, mi_ref, ms_ref, y_ref, v_ref, ty_ref, tv_ref, a2_ref, raw2_ref) = refs
    me = lax.axis_index("date")
    chunk = plan.chunk(me)
    nt = (((1,), (1,)), ((), ()))
    rows = [slice(b, b + 40) for b in range(0, DATES, 40)]
    sub = lax.broadcasted_iota(jnp.int32, (groups, LANES), 0)
    lane = lax.broadcasted_iota(jnp.int32, (groups, LANES), 1)
    diag = jnp.where(lane // pix == sub, 1.0, 0.0).astype(f32)

    spot = lax.broadcasted_iota(jnp.int32, (16, PART), 1)
    if plan.halves == 1:
        layout = [(0, span, 0)]
    elif last:
        layout = [(0, 2 * RIM, plan.pix), (plan.tail - plan.pieces[1][0], pix, jnp.where(plan.swapped(chunk), 0, span))]
    else:
        layout = [(0, pix, jnp.where(plan.swapped(chunk), span, 0)), (plan.pieces[1][0], 2 * RIM, plan.pix)]
    column = jnp.full((16, PART), -LANES, jnp.int32)
    for base, wide, col in layout:
        for line in range(LINES):
            start = base + line * wide
            column = jnp.where((spot >= start) & (spot < start + wide), spot - start + col, column)
    column = column - plan.half(chunk, slot) * pix
    offset = column - lax.rem(lax.broadcasted_iota(jnp.int32, (16, PART), 0), pix)
    inside = jnp.where((offset >= 0) & (offset <= 2 * RIM), 1.0, 0.0).astype(f32)
    mask = jnp.concatenate([inside, inside], axis=1).astype(bf16)
    rep = jnp.concatenate([inside] * (LANES // 16), axis=0).astype(bf16)

    def to_rows(y):
        return [
            jnp.sum(y[b * groups : (b + 1) * groups] * diag, axis=0, keepdims=True) for b in range(blocks)
        ]

    for r in range(n_date):
        for part in range(2):
            s = main[r][:, part * plan.stride : (part + 1) * plan.stride].astype(f32)
            if slot:
                s = pltpu.roll(s, plan.stride - plan.pieces[1][0], 1)
            s_ref[r * own : (r + 1) * own, part * PART : (part + 1) * PART] = s[:, 0:PART]
    if last:
        is_left = plan.swapped(chunk)
        depth = jnp.where(is_left, chunk, n_date - 1 - chunk)
        missing = RIM - depth * plan.cols
        wide, lanes = plan.tail_width, plan.tail_lanes
        base = plan.tail - plan.pieces[1][0] if plan.halves == 2 else 0

        @pl.when(missing > 0)
        def _():
            at = lax.broadcasted_iota(jnp.int32, (1, lanes), 1) + (PART - lanes - base)
            col = at
            for _line in range(1, LINES):
                col = jnp.where(col >= wide, col - wide, col)
            low = jnp.where(is_left, 0, wide - missing)
            valid = (col >= low) & (col < low + missing) & (at >= 0) & (at < LINES * wide)
            outermost = lax.axis_index("space") == jnp.where(is_left, 0, lax.axis_size("space") - 1)
            shift = jnp.where(is_left, missing - wide, wide - missing) + base + lanes
            for part in range(2):
                got = edge_ref[:, part * lanes : (part + 1) * lanes].astype(f32)
                got = jnp.where(outermost, 0.0, pltpu.roll(got, lax.rem(shift, lanes), 1))
                at_part = slice((part + 1) * PART - lanes, (part + 1) * PART)
                s_ref[:, at_part] = jnp.where(valid, got, s_ref[:, at_part])

    sr, si = s_ref[:, 0:PART], s_ref[:, PART : 2 * PART]
    left_ref[0:DATES, 0:PART] = sr.astype(bf16)
    left_ref[0:DATES, PART : 2 * PART] = si.astype(bf16)
    left_ref[DATES : 2 * DATES, 0:PART] = si.astype(bf16)
    left_ref[DATES : 2 * DATES, PART : 2 * PART] = (-sr).astype(bf16)
    left_ref[:, 2 * PART :] = left_ref[:, : 2 * PART]
    intensity = sr * sr + si * si
    weight = 1.0 / (jnp.sum(intensity, axis=0, keepdims=True) / DATES + epsilon)
    for part, s in enumerate((sr, si)):
        at = slice(part * PART, (part + 1) * PART)
        scaled = s * weight
        high = scaled.astype(bf16).astype(f32)
        high_ref[:, at] = high
        low_ref[:, at] = scaled - high
    weighted = intensity * weight
    high = weighted.astype(bf16)
    low = (weighted - high.astype(f32)).astype(bf16)
    power = lax.dot_general(high, rep, nt, preferred_element_type=f32)
    power = power + lax.dot_general(low, rep, nt, preferred_element_type=f32)
    root = lax.rsqrt(power + epsilon)
    for k in range(2):
        y = taper_ref[k] * root
        ty_ref[k] = y
        for b, row in enumerate(to_rows(y)):
            tv_ref[k, b : b + 1, :] = row

    unit = max(1, 16 // pix)

    def build(first, a_ref):
        for p in range(per):
            for g in range(0, groups, unit):
                for k, ref in enumerate((high_ref, low_ref)):
                    rows16 = jnp.concatenate(
                        [
                            jnp.broadcast_to(ref[pl.ds((first + p) * groups + g + u, 1), :], (pix, 2 * PART))
                            for u in range(unit)
                        ],
                        axis=0,
                    )
                    at = p * LANES + g * pix
                    a_ref[at : at + 16, k * 2 * PART : (k + 1) * 2 * PART] = rows16.astype(bf16) * mask

    def multiply(a_ref, raw_ref):
        raw_ref[...] = lax.dot_general(left_ref[...], a_ref[...], nt, preferred_element_type=f32)

    def normalise(first, raw_ref):
        for p in range(per):
            b = first + p
            grow_row = tv_ref[0, pl.ds(b, 1), :]
            decay_row = tv_ref[1, pl.ds(b, 1), :]
            at = slice(p * LANES, (p + 1) * LANES)
            sum_r = jnp.zeros((8, LANES), f32)
            sum_i = jnp.zeros((8, LANES), f32)
            for part in rows:
                shifted = slice(part.start + DATES, part.stop + DATES)
                factor = jnp.minimum(ty_ref[0, part] * decay_row, ty_ref[1, part] * grow_row)
                cr = raw_ref[part, at] * factor
                ci = raw_ref[shifted, at] * factor
                square = cr * cr + ci * ci
                cr_ref[b, part, :] = cr
                ci_ref[b, part, :] = ci
                ca_ref[b, part, :] = square * lax.rsqrt(jnp.maximum(square, 1e-36))
                sum_r = sum_r + jnp.sum(cr.reshape(5, 8, LANES), axis=0)
                sum_i = sum_i + jnp.sum(ci.reshape(5, 8, LANES), axis=0)
            at = pl.ds(pl.multiple_of(b * groups, groups), groups)
            y_ref[0, at] = jnp.sum(sum_r, axis=0, keepdims=True) * diag
            y_ref[1, at] = -jnp.sum(sum_i, axis=0, keepdims=True) * diag


    steps = blocks // per

    def coherence(pair, carry):
        step = 2 * pair
        multiply(a2_ref, raw2_ref)
        build((step + 2) * per, a_ref)
        normalise(step * per, raw_ref)
        multiply(a_ref, raw_ref)
        build(jnp.minimum(step + 3, steps - 1) * per, a2_ref)
        normalise((step + 1) * per, raw2_ref)
        return carry

    build(0, a_ref)
    multiply(a_ref, raw_ref)
    build(per, a2_ref)
    for pair in range((steps - 1) // 2):
        coherence(pair, 0)
    if steps % 2 == 0:
        multiply(a2_ref, raw2_ref)
        normalise((steps - 2) * per, raw_ref)
        normalise((steps - 1) * per, raw2_ref)
    else:
        normalise((steps - 1) * per, raw_ref)

    def unit_vector(scale):
        yr = group_sum(y_ref[0], pix) * scale
        yi = group_sum(y_ref[1], pix) * scale
        mean = jnp.sum(yr * yr + yi * yi, axis=0, keepdims=True) / DATES
        inv = lax.rsqrt(mean + epsilon)
        y_ref[0] = yr * inv
        y_ref[1] = yi * inv

    def first_step():
        yr, yi = y_ref[0], y_ref[1]
        square = yr * yr + yi * yi
        y_ref[2] = square * lax.rsqrt(jnp.maximum(square, 1e-36))
        for k in range(3):
            for b, row in enumerate(to_rows(y_ref[k])):
                v_ref[k, b : b + 1, :] = row

        def body(b, carry):
            la = v_ref[2, pl.ds(b, 1), :] * reweight_gain
            lr4 = v_ref[0, pl.ds(b, 1), :] * reweight_gain
            li4 = v_ref[1, pl.ds(b, 1), :] * reweight_gain
            sum_r = jnp.zeros((8, LANES), f32)
            sum_i = jnp.zeros((8, LANES), f32)
            for part in rows:
                cr, ci = cr_ref[b, part, :], ci_ref[b, part, :]
                yr, yi = y_ref[0, part], y_ref[1, part]
                pr = cr * yr + ci * yi
                pi = cr * yi - ci * yr
                den = (1.0 + ca_ref[b, part, :] * (y_ref[2, part] * la)) - (lr4 * pr + li4 * pi)
                g = 1.0 / den
                mr, mi = cr * g, ci * g
                mr_ref[b, part, :] = mr
                mi_ref[b, part, :] = mi
                ms_ref[b, part, :] = mr + mi
                sum_r = sum_r + jnp.sum((pr * g).reshape(5, 8, LANES), axis=0)
                sum_i = sum_i + jnp.sum((pi * g).reshape(5, 8, LANES), axis=0)
            set_row(b, jnp.sum(sum_r, axis=0, keepdims=True), jnp.sum(sum_i, axis=0, keepdims=True))
            return carry

        lax.fori_loop(0, blocks, body, 0, unroll=4 if blocks % 4 == 0 else 2)

    def set_row(b, vr, vi):
        tv_ref[0, pl.ds(b, 1), :] = vr
        tv_ref[1, pl.ds(b, 1), :] = vi

    def rows_to_lanes():
        vr, vi = tv_ref[0], tv_ref[1]
        v_ref[0] = vr
        v_ref[1] = vi - vr
        v_ref[2] = vr + vi
        for part in rows:
            zero = jnp.zeros((40, LANES), f32)

            def body(b, acc, part=part):
                v0, v1, v2 = (v_ref[k, pl.ds(b, 1), :] for k in range(3))
                return (
                    acc[0] + ms_ref[b, part, :] * v0,
                    acc[1] + mr_ref[b, part, :] * v1,
                    acc[2] + mi_ref[b, part, :] * v2,
                )

            k1, k2, k3 = lax.fori_loop(0, blocks, body, (zero, zero, zero), unroll=10)
            y_ref[0, part] = k1 - k3
            y_ref[1, part] = k1 + k2

    def lanes_to_rows():
        yr = group_sum(y_ref[0], pix)
        yi = group_sum(y_ref[1], pix)
        y_ref[0] = yr
        y_ref[1] = yi - yr
        y_ref[2] = yr + yi

        def body(step, carry):
            sums = [[jnp.zeros((8, LANES), f32) for _ in range(3)] for _ in range(per)]
            for part in rows:
                y0, y1, y2 = (y_ref[k, part] for k in range(3))
                for p in range(per):
                    b = step * per + p
                    for k, (m, y) in enumerate(((ms_ref, y0), (mi_ref, y1), (mr_ref, y2))):
                        sums[p][k] += jnp.sum((m[b, part, :] * y).reshape(5, 8, LANES), axis=0)
            for p in range(per):
                k1, k2, k3 = (jnp.sum(s, axis=0, keepdims=True) for s in sums[p])
                set_row(step * per + p, k1 + k2, k3 - k1)
            return carry

        lax.fori_loop(0, blocks // per, body, 0, unroll=2 if blocks // per % 2 == 0 else 1)

    unit_vector(1.0)
    for outer in range(ITERS):
        first_step()
        for step in range(1, POWER):
            if step % 2:
                rows_to_lanes()
            else:
                lanes_to_rows()
        unit_vector(1.0 / math.sqrt(DATES) ** POWER)

    if not last:
        outs[0][...] = y_ref[0:2]
        return
    lane_row = lax.broadcasted_iota(jnp.int32, (1, LANES), 1)
    here = lax.rem(lane_row // pix, plan.halves) == plan.half(chunk, slot)
    quarter = lane_row // (LANES // 4)
    for r in range(n_date):
        value = None
        for q in range(4):
            start = (n_date - r) % n_date * own + q % 2 * (own // 2)
            at = slice(start, start + own // 2)
            piece = y_ref[q // 2, at]
            if slot:
                piece = jnp.where(here, piece, before_ref[q // 2, at])
            value = piece if value is None else jnp.where(quarter == q, piece, value)
        outs[r][...] = value


def link(plan, slot, main, taper, *more):
    last = slot == plan.halves - 1
    matrix = pltpu.VMEM((plan.blocks, DATES, LANES), f32)
    samples = pltpu.VMEM((DATES, 2 * PART), f32)
    if last:
        shapes = [jax.ShapeDtypeStruct((plan.own // 2, LANES), f32)] * plan.n_date
    else:
        shapes = [jax.ShapeDtypeStruct((2, DATES, LANES), f32)]
    return pl.pallas_call(
        functools.partial(link_kernel, plan, slot),
        out_shape=shapes,
        in_specs=[VMEM] * (plan.n_date + 1 + len(more)),
        out_specs=[VMEM] * len(shapes),
        scratch_shapes=[
            samples,
            pltpu.VMEM((2 * DATES, 4 * PART), bf16),
            samples,
            samples,
            pltpu.VMEM((plan.per * LANES, 4 * PART), bf16),
            pltpu.VMEM((2 * DATES, PART), f32),
        ]
        + [matrix] * 6
        + [
            pltpu.VMEM((3, DATES, LANES), f32),
            pltpu.VMEM((3, plan.blocks, LANES), f32),
            pltpu.VMEM((2, DATES, LANES), f32),
            pltpu.VMEM((2, plan.blocks, LANES), f32),
            pltpu.VMEM((plan.per * LANES, 4 * PART), bf16),
            pltpu.VMEM((2 * DATES, PART), f32),
        ],
        compiler_params=pltpu.CompilerParams(vmem_limit_bytes=24 * 2**20),
    )(*main, taper, *more)


def local(acquisitions, acquisition_day):
    n_date, n_space = lax.axis_size("date"), lax.axis_size("space")
    plan = Plan(acquisitions.shape, n_date)
    own = plan.own

    samples = jnp.transpose(acquisitions, (0, 2, 1, 3))
    message = jax.ShapeDtypeStruct((own, 2 * plan.stride), bf16)
    plane = pltpu.VMEM((2, LINES, own, LANES), f32)
    params = pltpu.CompilerParams(vmem_limit_bytes=24 * 2**20)
    sent = pl.pallas_call(
        functools.partial(pack_kernel, plan, list(range(1, n_date))),
        out_shape=[message] * (n_date - 1),
        in_specs=[VMEM],
        out_specs=[VMEM] * (n_date - 1),
        scratch_shapes=[plane],
        compiler_params=params,
    )(samples)
    first, acquisition_day = lax.optimization_barrier((sent[0], acquisition_day))
    own_main, taper = pl.pallas_call(
        functools.partial(own_kernel, plan),
        out_shape=[message, jax.ShapeDtypeStruct((2, DATES, LANES), f32)],
        in_specs=[VMEM, VMEM],
        out_specs=[VMEM, VMEM],
        scratch_shapes=[plane],
        compiler_params=params,
    )(samples, acquisition_day)
    main = [own_main, first, *sent[1:]]
    main[0], taper = lax.optimization_barrier((main[0], taper))
    for r in range(1, n_date):
        main[r] = lax.ppermute(main[r], "date", [(i, (i + r) % n_date) for i in range(n_date)])
    swap = []
    for s in range(n_space - 1):
        for d in plan.right if s % 2 == 0 else plan.left:
            before, after = s * n_date + d, (s + 1) * n_date + d
            swap += [(before, after), (after, before)]
    idle = [d for d in range(n_date) if d not in plan.left + plan.right]
    for d in plan.left:
        swap += [(d, (n_space - 1) * n_date + d), ((n_space - 1) * n_date + d, d)]
    for s in range(n_space):
        for one, two in zip(idle[0::2], idle[1::2]):
            swap += [(s * n_date + one, s * n_date + two), (s * n_date + two, s * n_date + one)]
    edge = jnp.concatenate(
        [
            jnp.concatenate([m[:, k * plan.stride + plan.tail : (k + 1) * plan.stride] for k in range(2)], axis=1)
            for m in main
        ],
        axis=0,
    )
    edge = lax.ppermute(edge, ("space", "date"), swap)

    if plan.halves == 1:
        out = link(plan, 0, main, taper, edge)
    else:
        (before,) = link(plan, 0, main, taper)
        out = link(plan, 1, main, taper, edge, before)

    pieces = list(out)
    for k in range(1, n_date):
        pieces[k] = lax.ppermute(out[k], "date", [(i, (i + k) % n_date) for i in range(n_date)])
    return pl.pallas_call(
        functools.partial(unpack_kernel, plan),
        out_shape=jax.ShapeDtypeStruct((2, own, plan.width), f32),
        in_specs=[VMEM] * n_date,
        out_specs=VMEM,
        compiler_params=pltpu.CompilerParams(vmem_limit_bytes=24 * 2**20),
    )(*pieces)


def solution(mesh):
    return jax.shard_map(
        local,
        mesh=mesh,
        in_specs=(P(None, "date", None, "space"), P()),
        out_specs=P(None, "date", "space"),
        check_vma=False,
    )
```
